128 devices in a mesh: ctx: 32 (over y, x, core), grp: 4 (over z).
Axes of the slice: x: 4, y: 4, z: 4, core: 2. Of those that a mesh axis runs over, the one named last changes fastest.
Arguments:
- query_rows: bfloat16 [32768, 1024], P(('ctx', 'grp')), may hold values from -6 to 6
- key_rows: bfloat16 [32768, 1024], P(('ctx', 'grp')), may hold values from -6 to 6
- value_rows: bfloat16 [32768, 2048], P(('ctx', 'grp')), may hold values from -6 to 6
- log_decay: float32 [16, 32768], P(None, ('ctx', 'grp')), may hold values from -2 to 0, as said below
- beta_logit: float32 [16, 32768], P(None, ('ctx', 'grp')), may hold values from -8 to 6
- grad_out: bfloat16 [32768, 2048], P(('ctx', 'grp')), may hold values from -6 to 6
Outputs:
- layer_out: float32 [32768, 2048], P(('ctx', 'grp'))
- grad_query: float32 [32768, 1024], P(('ctx', 'grp'))
- grad_key: float32 [32768, 1024], P(('ctx', 'grp'))
- grad_value: float32 [32768, 2048], P(('ctx', 'grp'))
- grad_decay: float32 [16, 32768], P(None, ('ctx', 'grp'))
- grad_beta: float32 [16, 32768], P(None, ('ctx', 'grp'))
The draws below stay inside these ranges and needn't reach their ends.
Inputs may be any that keep to these rules, and one draw needn't show every extreme that they name: `log_decay`: every entry is negative.
All inputs are finite; a program needn't handle non-finite values.
Results may differ from the reference program's by a relative error of at most 0.00035.
Values sent between devices are 32-bit elements; how exact they have to be, the bound alone decides.
A program may use at most 192 MiB of HBM per device.

```python
import math
import jax
import jax.numpy as jnp
from jax import lax

DK = 128
DV = 128
VALUE_HEADS_HALF = 16
KEY_HEADS = 8
TOK_DEV = 256
SEQUENCE_TOKENS = 32768


def quick_heads(key, quick_count):
    ranking = jax.random.permutation(jax.random.fold_in(key, 7), VALUE_HEADS_HALF)
    return ranking < quick_count


def draw_log_decay(key, part):
    random_subkeys = jax.random.split(jax.random.fold_in(key, 13), 5)
    quick_count = VALUE_HEADS_HALF // 2
    quick_mask = quick_heads(key, quick_count)
    base_rate = jnp.where(quick_mask, 6.0 / TOK_DEV, 0.4 / SEQUENCE_TOKENS)[:, None]
    blocks = SEQUENCE_TOKENS // TOK_DEV
    halving = math.log(2.0)
    lowest = math.log(100.0)
    position = jax.random.uniform(random_subkeys[1], (VALUE_HEADS_HALF, blocks), jnp.float32, 0.0, 1.0)
    quick_log = -lowest + position * (lowest + halving)
    slow_log = -halving + position * (2.0 * halving)
    device_factor = jnp.exp(jnp.where(quick_mask[:, None], quick_log, slow_log))
    device_factor = jnp.repeat(device_factor, TOK_DEV, axis=1)
    roughness = jnp.exp(jax.random.uniform(random_subkeys[2], (VALUE_HEADS_HALF, SEQUENCE_TOKENS), jnp.float32, -halving, halving))
    decay_rates = base_rate * device_factor * roughness
    spike_locations = jax.random.randint(random_subkeys[3], (VALUE_HEADS_HALF, 2), 0, SEQUENCE_TOKENS)
    spike_depth = jax.random.uniform(random_subkeys[4], (VALUE_HEADS_HALF, 2), jnp.float32, 0.22, 0.41)
    token_positions = jnp.arange(SEQUENCE_TOKENS, dtype=jnp.int32)
    spike_hits = (token_positions[None, None, :] == spike_locations[:, :, None]).astype(jnp.float32)
    spike_events = jnp.sum(spike_hits * spike_depth[:, :, None], axis=1)
    return (-(decay_rates + spike_events)).astype(jnp.float32)


def draw_beta_logit(key, part):
    quick_count = VALUE_HEADS_HALF // 2
    quick_mask = quick_heads(key, quick_count)
    quick_key = jax.random.fold_in(key, 23)
    slow_key = jax.random.fold_in(key, 29)
    quick_logit = jnp.clip(1.5 * jax.random.normal(quick_key, (VALUE_HEADS_HALF, SEQUENCE_TOKENS), jnp.float32), -6.0, 6.0)
    slow_strength = 0.013
    slow_center = math.log(slow_strength / (1.0 - slow_strength))
    slow_logit = slow_center + jax.random.uniform(slow_key, (VALUE_HEADS_HALF, SEQUENCE_TOKENS), jnp.float32, -0.35, 0.35)
    return jnp.where(quick_mask[:, None], quick_logit, slow_logit).astype(jnp.float32)


def shard_levels(rng, extent, cuts, least, top_value):
    loudness = 1.0
    for axis_at, blocks in cuts:
        steps = jax.random.uniform(jax.random.fold_in(jax.random.fold_in(rng, 6), axis_at), (blocks,), jnp.float32, least / len(cuts), top_value / len(cuts))
        loudness = loudness * jnp.repeat(jnp.exp(steps), extent[axis_at] // blocks).reshape((-1,) + (1,) * (len(extent) - 1 - axis_at))
    return loudness


def bell_draw(key, dims, scale, limit, shards=(), held_as=jnp.bfloat16):
    drawn = jax.random.normal(key, dims, jnp.float32) * scale
    if len(shards) > 0:
        drawn = shard_levels(key, dims, shards, -0.22, 0.18) * drawn
    return jnp.clip(drawn, min=-limit, max=limit).astype(held_as)


def setup_inputs(seed: int = 0) -> dict:
    key_of = jax.random.split(jax.random.key(seed), 7)
    query_rows = bell_draw(key_of[0], (SEQUENCE_TOKENS, KEY_HEADS * DK), 1.0, 6.0, ((0, 128),))
    key_rows = bell_draw(key_of[1], (SEQUENCE_TOKENS, KEY_HEADS * DK), 1.0, 6.0, ((0, 128),))
    value_rows = bell_draw(key_of[2], (SEQUENCE_TOKENS, VALUE_HEADS_HALF * DV), 1.0, 6.0, ((0, 128),))
    log_decay = draw_log_decay(jax.random.fold_in(key_of[6], 71), 0)
    beta_logit = draw_beta_logit(jax.random.fold_in(key_of[6], 71), 0)
    grad_out = bell_draw(key_of[5], (SEQUENCE_TOKENS, VALUE_HEADS_HALF * DV), 1.0, 6.0, ((0, 128),))
    return dict(query_rows=query_rows, key_rows=key_rows, value_rows=value_rows, log_decay=log_decay, beta_logit=beta_logit, grad_out=grad_out)


exact_mode = lax.Precision.HIGHEST

def contract(pattern, former, latter):
    return jnp.einsum(pattern, former, latter, precision=exact_mode)

def unit_heads(matrix, heads_in, head_size):
    length = matrix.shape[0]
    shaped = matrix.reshape(length, heads_in, head_size)
    shaped = shaped * lax.rsqrt(lax.optimization_barrier(jnp.sum(shaped * shaped, axis=-1, keepdims=True)) + 1e-06)
    shaped = jnp.repeat(shaped, VALUE_HEADS_HALF // heads_in, axis=1)
    return shaped.transpose(1, 0, 2)

def prepare(query_part, key_part, value_part, rate_part, gate_part):
    length = query_part.shape[0]
    queries_n = unit_heads(query_part, KEY_HEADS, DK)
    keys_n = unit_heads(key_part, KEY_HEADS, DK)
    values_h = value_part.reshape(length, VALUE_HEADS_HALF, DV).transpose(1, 0, 2)
    strength = jax.nn.sigmoid(gate_part)
    running = jnp.cumsum(rate_part, axis=1)
    row_index = lax.broadcasted_iota(jnp.int32, (length, length), 0)
    column_index = lax.broadcasted_iota(jnp.int32, (length, length), 1)
    within = row_index >= column_index
    before = row_index > column_index
    spread = running[:, :, None] - running[:, None, :]
    decay_within = jnp.where(within, jnp.exp(jnp.where(within, spread, 0.0)), 0.0)
    decay_before = jnp.where(before, decay_within, 0.0)
    system = strength[:, :, None] * decay_before * contract('htd,hsd->hts', keys_n, keys_n)
    system = system + jnp.eye(length, dtype=jnp.float32)
    mixing = contract('htd,hsd->hts', queries_n, keys_n) * decay_within
    return (queries_n, keys_n, values_h, strength, running, system, mixing)

def block_step(query_part, key_part, value_part, rate_part, gate_part, carried):
    length = query_part.shape[0]
    queries_n, keys_n, values_h, strength, running, system, mixing = prepare(query_part, key_part, value_part, rate_part, gate_part)
    growth = jnp.exp(running)
    target = strength[:, :, None] * (values_h - growth[:, :, None] * contract('htd,hde->hte', keys_n, carried))
    written = jax.scipy.linalg.solve_triangular(system, target, lower=True, unit_diagonal=True)
    outputs = growth[:, :, None] * contract('htd,hde->hte', queries_n, carried) + contract('hts,hse->hte', mixing, written)
    fading = jnp.exp(running[:, -1:] - running)
    final_state = growth[:, -1][:, None, None] * carried + contract('hsd,hse->hde', fading[:, :, None] * keys_n, written)
    return (outputs.transpose(1, 0, 2).reshape(length, VALUE_HEADS_HALF * DV), final_state)

def reference(query_rows, key_rows, value_rows, log_decay, beta_logit, grad_out):
    blocks = SEQUENCE_TOKENS // TOK_DEV

    def split_rows(matrix):
        return matrix.astype(jnp.float32).reshape(blocks, TOK_DEV, matrix.shape[1])

    def split_heads(matrix):
        return matrix.reshape(VALUE_HEADS_HALF, blocks, TOK_DEV).transpose(1, 0, 2)

    def join_rows(matrix):
        return matrix.reshape(SEQUENCE_TOKENS, matrix.shape[2])

    def join_heads(matrix):
        return matrix.transpose(1, 0, 2).reshape(VALUE_HEADS_HALF, SEQUENCE_TOKENS)

    def advance(carried, pieces):
        outputs, final_state = block_step(pieces[0], pieces[1], pieces[2], pieces[3], pieces[4], carried)
        return (final_state, outputs)

    def forward_all(query_all, key_all, value_all, rate_all, gate_all):
        initial = jnp.zeros((VALUE_HEADS_HALF, DK, DV), jnp.float32)
        _, outputs = lax.scan(jax.checkpoint(advance), initial, (query_all, key_all, value_all, rate_all, gate_all))
        return outputs
    outputs, pullback = jax.vjp(forward_all, split_rows(query_rows), split_rows(key_rows), split_rows(value_rows), split_heads(log_decay), split_heads(beta_logit))
    gradients = pullback(split_rows(grad_out))
    layer_out = outputs.reshape(SEQUENCE_TOKENS, VALUE_HEADS_HALF * DV)
    return (layer_out, join_rows(gradients[0]), join_rows(gradients[1]), join_rows(gradients[2]), join_heads(gradients[3]), join_heads(gradients[4]))
```

```python
import functools
import jax
import jax.numpy as jnp
from jax import lax
from jax.experimental import pallas as pl
from jax.experimental.pallas import tpu as pltpu
from jax.sharding import PartitionSpec as P

F32 = jnp.float32
BF16 = jnp.bfloat16
TOK = 256
D = 128
HEADS = 16
KHEADS = 8


def dg(a, b, ca, cb):
    return lax.dot_general(a, b, (((ca,), (cb,)), ((), ())), preferred_element_type=F32)


def split(x):
    hi = x.astype(BF16)
    return hi, (x - hi.astype(F32)).astype(BF16)


def dot3(a, b, ca, cb):
    return dg(a[0], b[0], ca, cb) + (dg(a[0], b[1], ca, cb) + dg(a[1], b[0], ca, cb))


def dot2l(a, b, ca, cb):
    return dg(a[0], b, ca, cb) + dg(a[1], b, ca, cb)


def dot2r(a, b, ca, cb):
    return dg(a, b[0], ca, cb) + dg(a, b[1], ca, cb)


def iota(shape, dim):
    return lax.broadcasted_iota(jnp.int32, shape, dim)


def cumulate(rows, tri):
    hi = rows.astype(BF16)
    rest = rows - hi.astype(F32)
    mid = rest.astype(BF16)
    low = (rest - mid.astype(F32)).astype(BF16)
    parts = jnp.concatenate([hi.astype(F32), mid.astype(F32), low.astype(F32), jnp.zeros((2, TOK), F32)], axis=0)
    got = dg(parts.astype(BF16), tri, 1, 0)
    return got[0:2] + (got[2:4] + got[4:6])


def invert(systems):
    n = len(systems)
    lane = iota((16, D), 1)
    row = iota((16, D), 0)
    block = lane // 16
    packed = []
    for mat in systems:
        got = jnp.where(block == 0, mat[0:16], 0.0)
        for i in range(1, 8):
            got = jnp.where(block == i, mat[16 * i : 16 * i + 16], got)
        packed.append(got)
    inv = [jnp.where(lane % 16 == row, 1.0, 0.0).astype(F32) for _ in range(n)]
    for m in range(15):
        index = block * 16 + m
        for c in range(n):
            column = jnp.take_along_axis(packed[c], index, axis=1, mode="promise_in_bounds")
            inv[c] = inv[c] - column * inv[c][m : m + 1, :]
    wide_r = iota((D, D), 0)
    wide_c = iota((D, D), 1)
    full = [
        jnp.concatenate([jnp.where(block == i, inv[c], 0.0) for i in range(8)], axis=0)
        for c in range(n)
    ]
    for b in (16, 32, 64):
        mask = (wide_r // (2 * b) == wide_c // (2 * b)) & (wide_r // b % 2 == 1) & (wide_c // b % 2 == 0)
        sides = [split(jnp.where(mask, systems[c], 0.0)) for c in range(n)]
        ts = [split(full[c]) for c in range(n)]
        inner = [split(dot3(sides[c], ts[c], 1, 0)) for c in range(n)]
        full = [full[c] - dot3(ts[c], inner[c], 1, 0) for c in range(n)]
    return full


def rows_to_cols(rows8):
    return jnp.concatenate([rows8] * 16, axis=0).T


def cols_to_rows(cols):
    lane = iota((TOK, D), 1)
    got = jnp.zeros((TOK, D), F32)
    for i, col in enumerate(cols):
        got = jnp.where(lane == i, col, got)
    return got.T


def phase1(q_ref, k_ref, v_ref, go_ref, ld_ref, bl_ref,
           tri_ref, t_ref, m_ref, gam_ref, u_ref, w_ref, r_ref, auxc_ref, end_ref):
    q = q_ref[...]
    k = k_ref[...]
    qf = q.astype(F32)
    kf = k.astype(F32)
    rq = lax.rsqrt(jnp.sum(qf * qf, axis=1, keepdims=True) + 1e-6)
    rk = lax.rsqrt(jnp.sum(kf * kf, axis=1, keepdims=True) + 1e-6)
    rk_row = cols_to_rows([rk])[0:1]
    t_i = iota((TOK, TOK), 0)
    s_i = iota((TOK, TOK), 1)
    upper = jnp.where(t_i <= s_i, 1.0, 0.0).astype(BF16)
    run = cumulate(ld_ref[0], upper)
    logit = bl_ref[0]
    beta_rows = 1.0 / (1.0 + jnp.exp(-logit))
    last = run[:, TOK - 1 : TOK]
    cols = rows_to_cols(jnp.concatenate([run, beta_rows, jnp.exp(run), jnp.exp(last - run)], axis=0))
    kk = dg(k, k, 1, 1)
    qk = dg(q, k, 1, 1)
    lane = iota((TOK, D), 1)
    auxc = jnp.where(lane == 8, rq, jnp.where(lane == 9, rk, cols))
    auxc_ref[0] = auxc
    within = t_i >= s_i
    systems = []
    for j in range(2):
        spread = jnp.where(within, cols[:, j : j + 1] - run[j : j + 1], -1e30)
        gam = jnp.exp(spread) * rk_row
        gam_ref[j] = gam
        mix = split(qk * gam * rq)
        m_ref[j, 0] = mix[0]
        m_ref[j, 1] = mix[1]
        sysm = jnp.where(t_i > s_i, kk * gam * (cols[:, 2 + j : 3 + j] * rk), 0.0)
        systems.append(sysm)
    blocks = []
    for j in range(2):
        blocks += [systems[j][:D, :D], systems[j][D:, D:]]
    inv = invert(blocks)
    eye = jnp.where(iota((D, D), 0) == iota((D, D), 1), 1.0, 0.0)
    for j in range(2):
        t11, t22 = inv[2 * j], inv[2 * j + 1]
        inner = dot3(split(systems[j][D:, :D]), split(t11), 1, 0)
        t21 = -dot3(split(t22), split(inner), 1, 0)
        whole = jnp.concatenate(
            [jnp.concatenate([t11, jnp.zeros((D, D), F32)], axis=1), jnp.concatenate([t21, t22], axis=1)], axis=0)
        tb = split(whole * beta_rows[j : j + 1])
        t_ref[j, 0] = tb[0]
        t_ref[j, 1] = tb[1]
        g = cols[:, 4 + j : 5 + j]
        f = cols[:, 6 + j : 7 + j]
        v = v_ref[:, j * D : (j + 1) * D]
        go = go_ref[:, j * D : (j + 1) * D]
        u = dot2l(tb, v, 1, 0)
        w = dot3(tb, split(kf * (g * rk)), 1, 0)
        ws = split(w)
        u_ref[j] = u
        w_ref[j, 0] = ws[0]
        w_ref[j, 1] = ws[1]
        frk = f * rk
        mix = (m_ref[j, 0], m_ref[j, 1])
        r = dot2l(mix, go, 0, 0)
        r_ref[j] = r
        whole_g = jnp.exp(last[j : j + 1])
        tri_ref[j, 0] = eye * whole_g - dot2r(k, split(w * frk), 0, 0)
        tri_ref[j, 1] = dot2l(split(u * frk), k, 0, 0)
        tri_ref[j, 2] = dot2l(split(go.astype(F32) * (g * rq)), q, 0, 0) - dot3(split(r), ws, 0, 0)
        end_ref[j] = jnp.broadcast_to(whole_g, (8, D))


def phase3(q_ref, k_ref, v_ref, go_ref, bl_ref, sg_ref, t_ref, m_ref, gam_ref, u_ref, w_ref, r_ref, auxc_ref, end_ref,
           out_ref, gq_ref, gk_ref, gv_ref, gd_ref, gb_ref):
    q = q_ref[...]
    k = k_ref[...]
    aux = auxc_ref[0]
    rq = aux[:, 8:9]
    rk = aux[:, 9:10]
    t_i = iota((TOK, TOK), 0)
    s_i = iota((TOK, TOK), 1)
    strict = t_i > s_i
    lower = jnp.where(t_i >= s_i, 1.0, 0.0).astype(BF16)
    eq = jnp.zeros((TOK, D), F32)
    ek = jnp.zeros((TOK, D), F32)
    dots = []
    ends = []
    for j in range(2):
        g = aux[:, 4 + j : 5 + j]
        f = aux[:, 6 + j : 7 + j]
        st = sg_ref[j, 0]
        gt = sg_ref[j, 1]
        ss = split(st)
        gs = split(gt)
        v = v_ref[:, j * D : (j + 1) * D]
        go = go_ref[:, j * D : (j + 1) * D]
        tb = (t_ref[j, 0], t_ref[j, 1])
        mix = (m_ref[j, 0], m_ref[j, 1])
        w = (w_ref[j, 0], w_ref[j, 1])
        frk = f * rk
        x = u_ref[j] - dot3(w, ss, 1, 1)
        xs = split(x)
        out = dot2r(q, ss, 1, 1) * (g * rq) + dot3(mix, xs, 1, 0)
        out_ref[:, j * D : (j + 1) * D] = out
        dx = r_ref[j] + dot2r(k, gs, 1, 1) * frk
        y = dot3(tb, split(dx), 0, 0)
        ys = split(y)
        gv_ref[:, j * D : (j + 1) * D] = y
        gam = gam_ref[j]
        p = split(jnp.where(strict, dot3(ys, xs, 1, 1) * gam * (-rk), 0.0))
        n = split(dot2r(go, xs, 1, 1) * gam * rq)
        eq += dot2l(n, k, 1, 0) + dot2r(go, ss, 1, 0) * (g * rq)
        ek += dot2l(p, k, 1, 0) + dot2l(p, k, 0, 0) + dot2l(n, q, 0, 0)
        ek += dot3(xs, gs, 1, 0) * frk - dot3(ys, ss, 1, 0) * (g * rk)
        dots.append(jnp.sum(go.astype(F32) * out - v.astype(F32) * y, axis=1, keepdims=True))
        dots.append(jnp.sum(y * x, axis=1, keepdims=True))
        st_end = st * end_ref[j][0:1] + dot2l(split(x * frk), k, 0, 0)
        ends.append(jnp.sum(gt * st_end, keepdims=True))
    rows = cols_to_rows([dots[0], dots[2], dots[1], dots[3]])
    suffix = cumulate(rows[0:2], lower)
    gd_ref[0] = suffix + jnp.concatenate(ends, axis=0)
    gb_ref[0] = jnp.exp(-bl_ref[0]) * rows[2:4]
    qf = q.astype(F32)
    kf = k.astype(F32)
    gq_ref[...] = eq - qf * (rq * rq * jnp.sum(qf * eq, axis=1, keepdims=True))
    gk_ref[...] = ek - kf * (rk * rk * jnp.sum(kf * ek, axis=1, keepdims=True))


def wide(width):
    return pl.BlockSpec((TOK, width), lambda i: (0, i))


def whole_spec():
    return pl.BlockSpec((1, 2, TOK), lambda i: (i, 0, 0))


def per_head(*shape):
    return pl.BlockSpec((2,) + shape, lambda i: (i,) + (0,) * len(shape))


SAVED = [
    ((2, TOK, TOK), BF16),
    ((2, TOK, TOK), BF16),
    ((TOK, TOK), F32),
    ((TOK, D), F32),
    ((2, TOK, D), BF16),
    ((TOK, D), F32),
]
AUX_SPEC = pl.BlockSpec((1, TOK, D), lambda i: (i, 0, 0))
PARAMS = dict(vmem_limit_bytes=56 * 1024 * 1024)


def run_phase1(q, k, v, go, ld, bl):
    return pl.pallas_call(
        phase1,
        grid=(KHEADS,),
        in_specs=[wide(D), wide(D), wide(2 * D), wide(2 * D), whole_spec(), whole_spec()],
        out_specs=[per_head(3, D, D)] + [per_head(*s) for s, _ in SAVED] + [AUX_SPEC, per_head(8, D)],
        out_shape=[jax.ShapeDtypeStruct((HEADS, 3, D, D), F32)]
        + [jax.ShapeDtypeStruct((HEADS,) + s, t) for s, t in SAVED]
        + [jax.ShapeDtypeStruct((KHEADS, TOK, D), F32), jax.ShapeDtypeStruct((HEADS, 8, D), F32)],
        compiler_params=pltpu.CompilerParams(**PARAMS),
        name="local_transitions",
    )(q, k, v, go, ld.reshape(KHEADS, 2, TOK), bl.reshape(KHEADS, 2, TOK))


def run_phase3(q, k, v, go, bl, sg, saved):
    *outs, gd, gb = pl.pallas_call(
        phase3,
        grid=(KHEADS,),
        in_specs=[wide(D), wide(D), wide(2 * D), wide(2 * D), whole_spec(), per_head(2, D, D)]
        + [per_head(*s) for s, _ in SAVED] + [AUX_SPEC, per_head(8, D)],
        out_specs=[wide(2 * D), wide(D), wide(D), wide(2 * D), whole_spec(), whole_spec()],
        out_shape=[
            jax.ShapeDtypeStruct((TOK, HEADS * D), F32),
            jax.ShapeDtypeStruct((TOK, KHEADS * D), F32),
            jax.ShapeDtypeStruct((TOK, KHEADS * D), F32),
            jax.ShapeDtypeStruct((TOK, HEADS * D), F32),
            jax.ShapeDtypeStruct((KHEADS, 2, TOK), F32),
            jax.ShapeDtypeStruct((KHEADS, 2, TOK), F32),
        ],
        compiler_params=pltpu.CompilerParams(**PARAMS),
        name="local_gradients",
    )(q, k, v, go, bl.reshape(KHEADS, 2, TOK), sg, *saved)
    return (*outs, gd.reshape(HEADS, TOK), gb.reshape(HEADS, TOK))


MESH = pl.DeviceIdType.MESH
NZ, NC, NX, NY = 4, 2, 4, 4
SHARE = HEADS // NZ
PAIR = SHARE // NC
HALF = D // 2


def join(early, late):
    ae, be, ce = early
    al, bl, cl = late
    als = split(al)
    cls = split(cl)
    left = (jnp.concatenate([als[0], cls[0]], axis=0), jnp.concatenate([als[1], cls[1]], axis=0))
    both = dot3(left, split(ae), 1, 0)
    return both[:D], dot3(split(be), als, 1, 1) + bl, both[D:] + ce


def join_all(parts):
    while len(parts) > 1:
        parts = [join(parts[i], parts[i + 1]) for i in range(0, len(parts), 2)]
    return parts[0]


def chain(parts, state, grad):
    split_a = [split(p[0]) for p in parts]
    states = [state]
    for i in range(len(parts) - 1):
        states.append(dot3(split(states[-1]), split_a[i], 1, 1) + parts[i][1])
    grads = [grad]
    for i in range(len(parts) - 1, 0, -1):
        grads.append(dot3(split(grads[-1]), split_a[i], 1, 0) + parts[i][2])
    return states, grads[::-1]


def scan_kernel(tri_ref, sg_ref, zin, cout, cin, xout, xin, yin, xdo, xdi, cdo, cdi, zdo,
                own, zs, zr, cs, cr, xs, xr, ys, yr, xds, xdr, cds, cdr, zds, zdr):
    ctx = lax.axis_index("ctx")
    z = lax.axis_index("grp")
    c = lax.rem(ctx, NC)
    x = lax.rem(lax.div(ctx, NC), NX)
    y = lax.div(ctx, NC * NX)
    oc = 1 - c

    def at(yy, xx, cc, zz):
        return ((yy * NX + xx) * NC + cc, zz)

    def zpeer(d):
        return lax.rem(z + d, NZ)

    def xpeer(d):
        return lax.rem(x + d, NX)

    def ypeer(d):
        return lax.rem(y + d, NY)

    barrier = pltpu.get_barrier_semaphore()
    peers = [at(y, x, c, zpeer(d)) for d in range(1, NZ)]
    peers += [at(y, x, oc, z)]
    peers += [at(y, xpeer(d), c, z) for d in range(1, NX)]
    peers += [at(ypeer(d), x, c, z) for d in range(1, NY)]
    for peer in peers:
        pl.semaphore_signal(barrier, inc=1, device_id=peer, device_id_type=MESH)
    pl.semaphore_wait(barrier, len(peers))

    def remote(src, dst, send, recv, peer):
        return pltpu.make_async_remote_copy(
            src_ref=src, dst_ref=dst, send_sem=send, recv_sem=recv, device_id=peer, device_id_type=MESH)

    def slot(i):
        return lax.rem(i + PAIR * oc, SHARE)

    def zcopy(d, i):
        to = zpeer(d)
        return remote(tri_ref.at[SHARE * to + slot(i)], zin.at[z, slot(i)], zs.at[d - 1, i], zr.at[d - 1, i],
                      at(y, x, c, to))

    mine = pltpu.make_async_copy(tri_ref.at[pl.ds(SHARE * z, SHARE)], zin.at[z], own.at[0])
    mine.start()

    def zstart(i, _):
        for d in (2, 1, 3):
            zcopy(d, i).start()
        return 0

    lax.fori_loop(0, SHARE, zstart, 0)
    mine.wait()

    def ccopy(i):
        return remote(cout.at[i], cin.at[c, i], cs.at[i], cr.at[i], at(y, x, oc, z))

    def zjoin(i):
        for d in range(1, NZ):
            zcopy(d, i).wait_recv()
        h = slot(i)
        return join_all([tuple(zin[m, h, p] for p in range(3)) for m in range(NZ)])

    def zaway(i, _):
        got = zjoin(i)
        for p in range(3):
            cout[i, p] = got[p]
        ccopy(i).start()
        return 0

    lax.fori_loop(0, PAIR, zaway, 0)

    def zhere(i, _):
        got = zjoin(i + PAIR)
        for p in range(3):
            cin[c, i, p] = got[p]
        return 0

    lax.fori_loop(0, PAIR, zhere, 0)

    for i in range(PAIR):
        ccopy(i).wait_recv()
        a, b, g = join_all([tuple(cin[m, i, p] for p in range(3)) for m in range(NC)])
        for half in range(2):
            to = 2 * i + half
            rows = slice(half * HALF, (half + 1) * HALF)
            xout[to, 0:D] = a
            xout[to, D : D + HALF] = b[rows]
            xout[to, D + HALF : 2 * D] = g[rows]

    def xcopy(d):
        return remote(xout.at[xpeer(d)], xin.at[x], xs.at[d - 1], xr.at[d - 1], at(y, xpeer(d), c, z))

    for d in (2, 1, 3):
        xcopy(d).start()
    xin[x] = xout[x]
    for d in range(1, NX):
        xcopy(d).wait_recv()

    def packed(ref, m):
        return ref[m, 0:D], ref[m, D : D + HALF], ref[m, D + HALF : 2 * D]

    row = join_all([packed(xin, m) for m in range(NX)])
    yin[y, 0:D] = row[0]
    yin[y, D : D + HALF] = row[1]
    yin[y, D + HALF : 2 * D] = row[2]

    def ycopy(d):
        return remote(yin.at[y], yin.at[y], ys.at[d - 1], yr.at[d - 1], at(ypeer(d), x, c, z))

    for d in (2, 1, 3):
        ycopy(d).start()
    for d in range(1, NY):
        ycopy(d).wait_recv()
    zero = jnp.zeros((HALF, D), F32)
    states, grads = chain([packed(yin, m) for m in range(NY)], zero, zero)
    state, grad = states[0], grads[0]
    for m in range(1, NY):
        state = jnp.where(y == m, states[m], state)
        grad = jnp.where(y == m, grads[m], grad)

    states, grads = chain([packed(xin, m) for m in range(NX)], state, grad)
    for m in range(NX):
        xdo[m, 0:HALF] = states[m]
        xdo[m, HALF:D] = grads[m]

    def xdcopy(d):
        return remote(xdo.at[xpeer(d)], xdi.at[x], xds.at[d - 1], xdr.at[d - 1], at(y, xpeer(d), c, z))

    for d in (2, 1, 3):
        xdcopy(d).start()
    xdi[x] = xdo[x]
    for d in range(1, NX):
        xdcopy(d).wait_recv()
    for i in range(PAIR):
        state = jnp.concatenate([xdi[2 * i, 0:HALF], xdi[2 * i + 1, 0:HALF]], axis=0)
        grad = jnp.concatenate([xdi[2 * i, HALF:D], xdi[2 * i + 1, HALF:D]], axis=0)
        states, grads = chain([tuple(cin[m, i, p] for p in range(3)) for m in range(NC)], state, grad)
        for m in range(NC):
            cdo[m, i, 0] = states[m]
            cdo[m, i, 1] = grads[m]

    cdcopy = remote(cdo.at[oc], cdi.at[c], cds, cdr, at(y, x, oc, z))
    cdcopy.start()
    cdi[c] = cdo[c]

    def zdcopy(d, h):
        to = zpeer(d)
        return remote(zdo.at[to, h], sg_ref.at[SHARE * z + h], zds.at[d - 1, h], zdr.at[d - 1, h], at(y, x, c, to))

    def zdown(core):
        def body(i, _):
            h = PAIR * core + i
            parts = [tuple(zin[m, h, p] for p in range(3)) for m in range(NZ)]
            states, grads = chain(parts, cdi[core, i, 0], cdi[core, i, 1])
            for m in range(NZ):
                zdo[m, h, 0] = states[m]
                zdo[m, h, 1] = grads[m]
            for d in (2, 1, 3):
                zdcopy(d, h).start()
            return 0

        lax.fori_loop(0, PAIR, body, 0)

    zdown(c)
    cdcopy.wait_recv()
    zdown(oc)
    mine = pltpu.make_async_copy(zdo.at[z], sg_ref.at[pl.ds(SHARE * z, SHARE)], own.at[1])
    mine.start()

    def zwait(i, _):
        for d in range(1, NZ):
            zcopy(d, i).wait_send()
            zdcopy(d, i).wait()
        return 0

    lax.fori_loop(0, SHARE, zwait, 0)
    for i in range(PAIR):
        ccopy(i).wait_send()
    for d in range(1, NX):
        xcopy(d).wait_send()
        xdcopy(d).wait_send()
    for d in range(1, NY):
        ycopy(d).wait_send()
    cdcopy.wait_send()
    mine.wait()


def run_scan(tri):
    dma = pltpu.SemaphoreType.DMA
    vm = lambda *shape: pltpu.VMEM(shape, F32)
    return pl.pallas_call(
        scan_kernel,
        in_specs=[pl.BlockSpec(memory_space=pl.ANY)],
        out_specs=pl.BlockSpec(memory_space=pl.ANY),
        out_shape=jax.ShapeDtypeStruct((HEADS, 2, D, D), F32),
        scratch_shapes=[
            vm(NZ, SHARE, 3, D, D), vm(PAIR, 3, D, D), vm(NC, PAIR, 3, D, D),
            vm(NX, 2 * D, D), vm(NX, 2 * D, D), vm(NY, 2 * D, D),
            vm(NX, D, D), vm(NX, D, D), vm(NC, PAIR, 2, D, D), vm(NC, PAIR, 2, D, D),
            vm(NZ, SHARE, 2, D, D),
            dma((2,)),
            dma((NZ - 1, SHARE)), dma((NZ - 1, SHARE)), dma((PAIR,)), dma((PAIR,)),
            dma((NX - 1,)), dma((NX - 1,)), dma((NY - 1,)), dma((NY - 1,)),
            dma((NX - 1,)), dma((NX - 1,)), dma, dma,
            dma((NZ - 1, SHARE)), dma((NZ - 1, SHARE)),
        ],
        compiler_params=pltpu.CompilerParams(collective_id=0, has_side_effects=True, **PARAMS),
        name="device_scan",
    )(tri)


def on_device(query_rows, key_rows, value_rows, log_decay, beta_logit, grad_out):
    tri, *saved = run_phase1(query_rows, key_rows, value_rows, grad_out, log_decay, beta_logit)
    sg = run_scan(tri)
    return run_phase3(query_rows, key_rows, value_rows, grad_out, beta_logit, sg, saved)


def solution(mesh):
    rows = P(("ctx", "grp"), None)
    heads = P(None, ("ctx", "grp"))
    return jax.shard_map(
        on_device,
        mesh=mesh,
        in_specs=(rows, rows, rows, heads, heads, rows),
        out_specs=(rows, rows, rows, rows, heads, heads),
        check_vma=False,
    )
```

```python
import jax
import jax.numpy as jnp
from jax import lax
from jax.experimental import pallas as pl
from jax.experimental.pallas import tpu as pltpu
from jax.sharding import PartitionSpec as P

F32 = jnp.float32
BF16 = jnp.bfloat16
TOK = 256
D = 128
HEADS = 16
KHEADS = 8


def dg(a, b, ca, cb):
    return lax.dot_general(a, b, (((ca,), (cb,)), ((), ())), preferred_element_type=F32)


def split(x):
    hi = x.astype(BF16)
    return hi, (x - hi.astype(F32)).astype(BF16)


def dot3(a, b, ca, cb):
    return dg(a[0], b[0], ca, cb) + (dg(a[0], b[1], ca, cb) + dg(a[1], b[0], ca, cb))


def dot2l(a, b, ca, cb):
    return dg(a[0], b, ca, cb) + dg(a[1], b, ca, cb)


def dot2r(a, b, ca, cb):
    return dg(a, b[0], ca, cb) + dg(a, b[1], ca, cb)


def iota(shape, dim):
    return lax.broadcasted_iota(jnp.int32, shape, dim)


def cumulate(rows, tri):
    hi = rows.astype(BF16)
    rest = rows - hi.astype(F32)
    mid = rest.astype(BF16)
    low = (rest - mid.astype(F32)).astype(BF16)
    parts = jnp.concatenate([hi.astype(F32), mid.astype(F32), low.astype(F32), jnp.zeros((2, TOK), F32)], axis=0)
    got = dg(parts.astype(BF16), tri, 1, 0)
    return got[0:2] + (got[2:4] + got[4:6])


def invert(systems):
    n = len(systems)
    lane = iota((16, D), 1)
    row = iota((16, D), 0)
    block = lane // 16
    packed = []
    for mat in systems:
        got = jnp.where(block == 0, mat[0:16], 0.0)
        for i in range(1, 8):
            got = jnp.where(block == i, mat[16 * i : 16 * i + 16], got)
        packed.append(got)
    inv = [jnp.where(lane % 16 == row, 1.0, 0.0).astype(F32) for _ in range(n)]
    for m in range(15):
        index = block * 16 + m
        for c in range(n):
            column = jnp.take_along_axis(packed[c], index, axis=1, mode="promise_in_bounds")
            inv[c] = inv[c] - column * inv[c][m : m + 1, :]
    wide_r = iota((D, D), 0)
    wide_c = iota((D, D), 1)
    full = [
        jnp.concatenate([jnp.where(block == i, inv[c], 0.0) for i in range(8)], axis=0)
        for c in range(n)
    ]
    for b in (16, 32, 64):
        mask = (wide_r // (2 * b) == wide_c // (2 * b)) & (wide_r // b % 2 == 1) & (wide_c // b % 2 == 0)
        sides = [split(jnp.where(mask, systems[c], 0.0)) for c in range(n)]
        ts = [split(full[c]) for c in range(n)]
        inner = [split(dot3(sides[c], ts[c], 1, 0)) for c in range(n)]
        full = [full[c] - dot3(ts[c], inner[c], 1, 0) for c in range(n)]
    return full


def rows_to_cols(rows8):
    return jnp.concatenate([rows8] * 16, axis=0).T


def cols_to_rows(cols):
    lane = iota((TOK, D), 1)
    got = jnp.zeros((TOK, D), F32)
    for i, col in enumerate(cols):
        got = jnp.where(lane == i, col, got)
    return got.T


VMEM_LIMIT = 60 * 1024 * 1024


def phase1(q_ref, k_ref, v_ref, go_ref, ld_ref, bl_ref,
           tri_ref, t_ref, m_ref, gam_ref, u_ref, w_ref, r_ref, auxc_ref, end_ref):
    q = q_ref[...]
    k = k_ref[...]
    qf = q.astype(F32)
    kf = k.astype(F32)
    rq = lax.rsqrt(jnp.sum(qf * qf, axis=1, keepdims=True) + 1e-6)
    rk = lax.rsqrt(jnp.sum(kf * kf, axis=1, keepdims=True) + 1e-6)
    rk_row = cols_to_rows([rk])[0:1]
    t_i = iota((TOK, TOK), 0)
    s_i = iota((TOK, TOK), 1)
    upper = jnp.where(t_i <= s_i, 1.0, 0.0).astype(BF16)
    run = cumulate(ld_ref[...], upper)
    logit = bl_ref[...]
    beta_rows = 1.0 / (1.0 + jnp.exp(-logit))
    last = run[:, TOK - 1 : TOK]
    cols = rows_to_cols(jnp.concatenate([run, beta_rows, jnp.exp(run), jnp.exp(last - run)], axis=0))
    kk = dg(k, k, 1, 1)
    qk = dg(q, k, 1, 1)
    lane = iota((TOK, D), 1)
    auxc = jnp.where(lane == 8, rq, jnp.where(lane == 9, rk, cols))
    auxc_ref[...] = auxc
    within = t_i >= s_i
    systems = []
    for j in range(2):
        spread = jnp.where(within, cols[:, j : j + 1] - run[j : j + 1], -1e30)
        gam = jnp.exp(spread) * rk_row
        gam_ref[j] = gam
        mix = split(qk * gam * rq)
        m_ref[j, 0] = mix[0]
        m_ref[j, 1] = mix[1]
        sysm = jnp.where(t_i > s_i, kk * gam * (cols[:, 2 + j : 3 + j] * rk), 0.0)
        systems.append(sysm)
    blocks = []
    for j in range(2):
        blocks += [systems[j][:D, :D], systems[j][D:, D:]]
    inv = invert(blocks)
    eye = jnp.where(iota((D, D), 0) == iota((D, D), 1), 1.0, 0.0)
    for j in range(2):
        t11, t22 = inv[2 * j], inv[2 * j + 1]
        inner = dot3(split(systems[j][D:, :D]), split(t11), 1, 0)
        t21 = -dot3(split(t22), split(inner), 1, 0)
        whole = jnp.concatenate(
            [jnp.concatenate([t11, jnp.zeros((D, D), F32)], axis=1), jnp.concatenate([t21, t22], axis=1)], axis=0)
        tb = split(whole * beta_rows[j : j + 1])
        t_ref[j, 0] = tb[0]
        t_ref[j, 1] = tb[1]
        g = cols[:, 4 + j : 5 + j]
        f = cols[:, 6 + j : 7 + j]
        v = v_ref[:, j * D : (j + 1) * D]
        go = go_ref[:, j * D : (j + 1) * D]
        u = dot2l(tb, v, 1, 0)
        w = dot3(tb, split(kf * (g * rk)), 1, 0)
        ws = split(w)
        u_ref[j] = u
        w_ref[j, 0] = ws[0]
        w_ref[j, 1] = ws[1]
        frk = f * rk
        mix = (m_ref[j, 0], m_ref[j, 1])
        r = dot2l(mix, go, 0, 0)
        r_ref[j] = r
        whole_g = jnp.exp(last[j : j + 1])
        tri_ref[j, 0] = eye * whole_g - dot2r(k, split(w * frk), 0, 0)
        tri_ref[j, 1] = dot2l(split(u * frk), k, 0, 0)
        tri_ref[j, 2] = dot2l(split(go.astype(F32) * (g * rq)), q, 0, 0) - dot3(split(r), ws, 0, 0)
        end_ref[j] = jnp.broadcast_to(whole_g, (8, D))


def phase3(q_ref, k_ref, v_ref, go_ref, bl_ref, sg_ref, t_ref, m_ref, gam_ref, u_ref, w_ref, r_ref, auxc_ref, end_ref,
           out_ref, gq_ref, gk_ref, gv_ref, gd_ref, gb_ref):
    q = q_ref[...]
    k = k_ref[...]
    aux = auxc_ref[...]
    rq = aux[:, 8:9]
    rk = aux[:, 9:10]
    t_i = iota((TOK, TOK), 0)
    s_i = iota((TOK, TOK), 1)
    strict = t_i > s_i
    lower = jnp.where(t_i >= s_i, 1.0, 0.0).astype(BF16)
    eq = jnp.zeros((TOK, D), F32)
    ek = jnp.zeros((TOK, D), F32)
    dots = []
    ends = []
    for j in range(2):
        g = aux[:, 4 + j : 5 + j]
        f = aux[:, 6 + j : 7 + j]
        st = sg_ref[j, 0]
        gt = sg_ref[j, 1]
        ss = split(st)
        gs = split(gt)
        v = v_ref[:, j * D : (j + 1) * D]
        go = go_ref[:, j * D : (j + 1) * D]
        tb = (t_ref[j, 0], t_ref[j, 1])
        mix = (m_ref[j, 0], m_ref[j, 1])
        w = (w_ref[j, 0], w_ref[j, 1])
        frk = f * rk
        x = u_ref[j] - dot3(w, ss, 1, 1)
        xs = split(x)
        out = dot2r(q, ss, 1, 1) * (g * rq) + dot3(mix, xs, 1, 0)
        out_ref[:, j * D : (j + 1) * D] = out
        dx = r_ref[j] + dot2r(k, gs, 1, 1) * frk
        y = dot3(tb, split(dx), 0, 0)
        ys = split(y)
        gv_ref[:, j * D : (j + 1) * D] = y
        gam = gam_ref[j]
        p = split(jnp.where(strict, dot3(ys, xs, 1, 1) * gam * (-rk), 0.0))
        n = split(dot2r(go, xs, 1, 1) * gam * rq)
        eq += dot2l(n, k, 1, 0) + dot2r(go, ss, 1, 0) * (g * rq)
        ek += dot2l(p, k, 1, 0) + dot2l(p, k, 0, 0) + dot2l(n, q, 0, 0)
        ek += dot3(xs, gs, 1, 0) * frk - dot3(ys, ss, 1, 0) * (g * rk)
        dots.append(jnp.sum(go.astype(F32) * out - v.astype(F32) * y, axis=1, keepdims=True))
        dots.append(jnp.sum(y * x, axis=1, keepdims=True))
        st_end = st * end_ref[j][0:1] + dot2l(split(x * frk), k, 0, 0)
        ends.append(jnp.sum(gt * st_end, keepdims=True))
    rows = cols_to_rows([dots[0], dots[2], dots[1], dots[3]])
    suffix = cumulate(rows[0:2], lower)
    gd_ref[...] = suffix + jnp.concatenate(ends, axis=0)
    gb_ref[...] = jnp.exp(-bl_ref[...]) * rows[2:4]
    qf = q.astype(F32)
    kf = k.astype(F32)
    gq_ref[...] = eq - qf * (rq * rq * jnp.sum(qf * eq, axis=1, keepdims=True))
    gk_ref[...] = ek - kf * (rk * rk * jnp.sum(kf * ek, axis=1, keepdims=True))


MESH = pl.DeviceIdType.MESH
NZ, NC, NX, NY = 4, 2, 4, 4
SHARE = HEADS // NZ
PAIR = SHARE // NC
HALF = D // 2


def join(early, late):
    ae, be, ce = early
    al, bl, cl = late
    als = split(al)
    cls = split(cl)
    left = (jnp.concatenate([als[0], cls[0]], axis=0), jnp.concatenate([als[1], cls[1]], axis=0))
    both = dot3(left, split(ae), 1, 0)
    return both[:D], dot3(split(be), als, 1, 1) + bl, both[D:] + ce


def join_all(parts):
    while len(parts) > 1:
        parts = [join(parts[i], parts[i + 1]) for i in range(0, len(parts), 2)]
    return parts[0]


def chain(parts, state, grad):
    split_a = [split(p[0]) for p in parts]
    states = [state]
    for i in range(len(parts) - 1):
        states.append(dot3(split(states[-1]), split_a[i], 1, 1) + parts[i][1])
    grads = [grad]
    for i in range(len(parts) - 1, 0, -1):
        grads.append(dot3(split(grads[-1]), split_a[i], 1, 0) + parts[i][2])
    return states, grads[::-1]


def place(i):
    own = lax.div(i, 6)
    r = lax.rem(i, 3)
    d = (1 - own) * lax.div(3 * r * r + 4 - 5 * r, 2)
    half = (1 - own) * lax.div(i, 3) + own * (i - 6)
    return d, half


def layer_kernel(q_hbm, k_hbm, v_hbm, go_hbm, ld_ref, bl_ref,
                 out_hbm, gq_hbm, gk_hbm, gv_hbm, gd_ref, gb_ref,
                 qb, kb, vb, gob, t_ref, m_ref, gam_ref, u_ref, w_ref, r_ref, aux_ref, end_ref,
                 tri, zin, cout, cin, xout, xin, yin, xdo, xdi, cdo, cdi, zdo, sgin,
                 outb, gqb, gkb, gvb,
                 ins, outs, zs, zr, cs, cr, xs, xr, ys, yr, xds, xdr, cds, cdr, zds, zdr):
    ctx = lax.axis_index("ctx")
    z = lax.axis_index("grp")
    c = lax.rem(ctx, NC)
    x = lax.rem(lax.div(ctx, NC), NX)
    y = lax.div(ctx, NC * NX)
    oc = 1 - c

    def at(yy, xx, cc, zz):
        return ((yy * NX + xx) * NC + cc, zz)

    def zpeer(d):
        return lax.rem(z + d, NZ)

    def xpeer(d):
        return lax.rem(x + d, NX)

    def ypeer(d):
        return lax.rem(y + d, NY)

    barrier = pltpu.get_barrier_semaphore()
    peers = [at(y, x, c, zpeer(d)) for d in range(1, NZ)]
    peers += [at(y, x, oc, z)]
    peers += [at(y, xpeer(d), c, z) for d in range(1, NX)]
    peers += [at(ypeer(d), x, c, z) for d in range(1, NY)]
    for peer in peers:
        pl.semaphore_signal(barrier, inc=1, device_id=peer, device_id_type=MESH)

    def up_step(i):
        d, half = place(i)
        core = lax.rem(oc + half, NC)
        return d, half, core, NC * zpeer(d) + core

    def down_step(i):
        d, half = place(lax.rem(i + 6, 8))
        core = lax.rem(c + half, NC)
        return d, half, core, NC * lax.rem(z + NZ - d, NZ) + core

    def loads(kh):
        one = pl.ds(pl.multiple_of(kh * D, D), D)
        two = pl.ds(pl.multiple_of(kh * 2 * D, 2 * D), 2 * D)
        return [
            pltpu.make_async_copy(q_hbm.at[:, one], qb.at[kh], ins.at[0, kh]),
            pltpu.make_async_copy(k_hbm.at[:, one], kb.at[kh], ins.at[1, kh]),
            pltpu.make_async_copy(v_hbm.at[:, two], vb.at[kh], ins.at[2, kh]),
            pltpu.make_async_copy(go_hbm.at[:, two], gob.at[kh], ins.at[3, kh]),
        ]

    def stores(kh):
        one = pl.ds(pl.multiple_of(kh * D, D), D)
        two = pl.ds(pl.multiple_of(kh * 2 * D, 2 * D), 2 * D)
        return [
            pltpu.make_async_copy(outb.at[kh], out_hbm.at[:, two], outs.at[0, kh]),
            pltpu.make_async_copy(gqb.at[kh], gq_hbm.at[:, one], outs.at[1, kh]),
            pltpu.make_async_copy(gkb.at[kh], gk_hbm.at[:, one], outs.at[2, kh]),
            pltpu.make_async_copy(gvb.at[kh], gv_hbm.at[:, two], outs.at[3, kh]),
        ]

    def load_start(i, _):
        for copy in loads(up_step(i)[3]):
            copy.start()
        return 0

    lax.fori_loop(0, KHEADS, load_start, 0)

    def remote(src, dst, send, recv, peer):
        return pltpu.make_async_remote_copy(
            src_ref=src, dst_ref=dst, send_sem=send, recv_sem=recv, device_id=peer, device_id_type=MESH)

    def zcopy(d, half):
        to = zpeer(d)
        core = lax.rem(oc + half, NC)
        return remote(tri.at[NC * to + core], zin.at[z, core], zs.at[d - 1, half], zr.at[d - 1, half],
                      at(y, x, c, to))

    def ccopy():
        return remote(cout, cin.at[c], cs, cr, at(y, x, oc, z))

    def zjoin(core, half, dst):
        for d in range(1, NZ):
            zcopy(d, half).wait_recv()
        for i in range(PAIR):
            got = join_all([tuple(zin[m, core, i, p] for p in range(3)) for m in range(NZ)])
            for p in range(3):
                dst[i, p] = got[p]

    pl.semaphore_wait(barrier, len(peers))

    def up(i, _):
        d, half, core, kh = up_step(i)
        for copy in loads(kh):
            copy.wait()
        pair = pl.ds(PAIR * kh, PAIR)
        phase1(qb.at[kh], kb.at[kh], vb.at[kh], gob.at[kh], ld_ref.at[kh], bl_ref.at[kh], tri.at[kh],
               t_ref.at[pair], m_ref.at[pair], gam_ref.at[pair], u_ref.at[pair], w_ref.at[pair], r_ref.at[pair],
               aux_ref.at[kh], end_ref.at[pair])

        @pl.when(i < 6)
        def _():
            zcopy(d, half).start()

        @pl.when(i >= 6)
        def _():
            zin[z, core] = tri[kh]

        @pl.when(i == 6)
        def _():
            zjoin(oc, 0, cout)
            ccopy().start()

        return 0

    lax.fori_loop(0, KHEADS, up, 0)
    zjoin(c, 1, cin.at[c])

    ccopy().wait_recv()
    for i in range(PAIR):
        a, b, g = join_all([tuple(cin[m, i, p] for p in range(3)) for m in range(NC)])
        for half in range(2):
            to = 2 * i + half
            rows = slice(half * HALF, (half + 1) * HALF)
            xout[to, 0:D] = a
            xout[to, D : D + HALF] = b[rows]
            xout[to, D + HALF : 2 * D] = g[rows]

    def xcopy(d):
        return remote(xout.at[xpeer(d)], xin.at[x], xs.at[d - 1], xr.at[d - 1], at(y, xpeer(d), c, z))

    for d in (2, 1, 3):
        xcopy(d).start()
    xin[x] = xout[x]
    for d in range(1, NX):
        xcopy(d).wait_recv()

    def packed(ref, m):
        return ref[m, 0:D], ref[m, D : D + HALF], ref[m, D + HALF : 2 * D]

    row = join_all([packed(xin, m) for m in range(NX)])
    yin[y, 0:D] = row[0]
    yin[y, D : D + HALF] = row[1]
    yin[y, D + HALF : 2 * D] = row[2]

    def ycopy(d):
        return remote(yin.at[y], yin.at[y], ys.at[d - 1], yr.at[d - 1], at(ypeer(d), x, c, z))

    for d in (2, 1, 3):
        ycopy(d).start()
    for d in range(1, NY):
        ycopy(d).wait_recv()
    zero = jnp.zeros((HALF, D), F32)
    states, grads = chain([packed(yin, m) for m in range(NY)], zero, zero)
    state, grad = states[0], grads[0]
    for m in range(1, NY):
        state = jnp.where(y == m, states[m], state)
        grad = jnp.where(y == m, grads[m], grad)

    states, grads = chain([packed(xin, m) for m in range(NX)], state, grad)
    for m in range(NX):
        xdo[m, 0:HALF] = states[m]
        xdo[m, HALF:D] = grads[m]

    def xdcopy(d):
        return remote(xdo.at[xpeer(d)], xdi.at[x], xds.at[d - 1], xdr.at[d - 1], at(y, xpeer(d), c, z))

    for d in (2, 1, 3):
        xdcopy(d).start()
    xdi[x] = xdo[x]
    for d in range(1, NX):
        xdcopy(d).wait_recv()
    for i in range(PAIR):
        state = jnp.concatenate([xdi[2 * i, 0:HALF], xdi[2 * i + 1, 0:HALF]], axis=0)
        grad = jnp.concatenate([xdi[2 * i, HALF:D], xdi[2 * i + 1, HALF:D]], axis=0)
        states, grads = chain([tuple(cin[m, i, p] for p in range(3)) for m in range(NC)], state, grad)
        for m in range(NC):
            cdo[m, i, 0] = states[m]
            cdo[m, i, 1] = grads[m]

    cdcopy = remote(cdo.at[oc], cdi.at[c], cds, cdr, at(y, x, oc, z))
    cdcopy.start()
    cdi[c] = cdo[c]

    def zdcopy(d, half):
        to = zpeer(d)
        core = lax.rem(c + half, NC)
        return remote(zdo.at[to, core], sgin.at[z, core], zds.at[d - 1, half], zdr.at[d - 1, half], at(y, x, c, to))

    def zdown(half, _):
        core = lax.rem(c + half, NC)

        @pl.when(half == 1)
        def _():
            cdcopy.wait_recv()

        for i in range(PAIR):
            parts = [tuple(zin[m, core, i, p] for p in range(3)) for m in range(NZ)]
            states, grads = chain(parts, cdi[core, i, 0], cdi[core, i, 1])
            for m in range(NZ):
                zdo[m, core, i, 0] = states[m]
                zdo[m, core, i, 1] = grads[m]
        for d in (2, 1, 3):
            zdcopy(d, half).start()
        sgin[z, core] = zdo[z, core]
        return 0

    lax.fori_loop(0, NC, zdown, 0)

    def down(i, _):
        d, half, core, kh = down_step(i)

        @pl.when(i >= 2)
        def _():
            zdcopy(d, half).wait_recv()

        pair = pl.ds(PAIR * kh, PAIR)
        phase3(qb.at[kh], kb.at[kh], vb.at[kh], gob.at[kh], bl_ref.at[kh], sgin.at[lax.div(kh, NC), core],
               t_ref.at[pair], m_ref.at[pair], gam_ref.at[pair], u_ref.at[pair], w_ref.at[pair], r_ref.at[pair],
               aux_ref.at[kh], end_ref.at[pair],
               outb.at[kh], gqb.at[kh], gkb.at[kh], gvb.at[kh], gd_ref.at[kh], gb_ref.at[kh])
        for copy in stores(kh):
            copy.start()
        return 0

    lax.fori_loop(0, KHEADS, down, 0)

    for half in range(2):
        for d in range(1, NZ):
            zcopy(d, half).wait_send()
            zdcopy(d, half).wait_send()
    ccopy().wait_send()
    for d in range(1, NX):
        xcopy(d).wait_send()
        xdcopy(d).wait_send()
    for d in range(1, NY):
        ycopy(d).wait_send()
    cdcopy.wait_send()

    def store_wait(kh, _):
        for copy in stores(kh):
            copy.wait()
        return 0

    lax.fori_loop(0, KHEADS, store_wait, 0)


def run_layer(q, k, v, go, ld, bl):
    dma = pltpu.SemaphoreType.DMA

    def vm(*shape, dtype=F32):
        return pltpu.VMEM(shape, dtype)

    hbm = pl.BlockSpec(memory_space=pl.ANY)
    vmem = pl.BlockSpec(memory_space=pltpu.VMEM)
    *outs, gd, gb = pl.pallas_call(
        layer_kernel,
        in_specs=[hbm] * 4 + [vmem] * 2,
        out_specs=[hbm] * 4 + [vmem] * 2,
        out_shape=[
            jax.ShapeDtypeStruct((TOK, HEADS * D), F32),
            jax.ShapeDtypeStruct((TOK, KHEADS * D), F32),
            jax.ShapeDtypeStruct((TOK, KHEADS * D), F32),
            jax.ShapeDtypeStruct((TOK, HEADS * D), F32),
            jax.ShapeDtypeStruct((KHEADS, 2, TOK), F32),
            jax.ShapeDtypeStruct((KHEADS, 2, TOK), F32),
        ],
        scratch_shapes=[
            vm(KHEADS, TOK, D, dtype=BF16), vm(KHEADS, TOK, D, dtype=BF16),
            vm(KHEADS, TOK, 2 * D, dtype=BF16), vm(KHEADS, TOK, 2 * D, dtype=BF16),
            vm(HEADS, 2, TOK, TOK, dtype=BF16), vm(HEADS, 2, TOK, TOK, dtype=BF16), vm(HEADS, TOK, TOK),
            vm(HEADS, TOK, D), vm(HEADS, 2, TOK, D, dtype=BF16), vm(HEADS, TOK, D),
            vm(KHEADS, TOK, D), vm(HEADS, 8, D),
            vm(KHEADS, PAIR, 3, D, D), vm(NZ, NC, PAIR, 3, D, D),
            vm(PAIR, 3, D, D), vm(NC, PAIR, 3, D, D),
            vm(NX, 2 * D, D), vm(NX, 2 * D, D), vm(NY, 2 * D, D),
            vm(NX, D, D), vm(NX, D, D), vm(NC, PAIR, 2, D, D), vm(NC, PAIR, 2, D, D),
            vm(NZ, NC, PAIR, 2, D, D), vm(NZ, NC, PAIR, 2, D, D),
            vm(KHEADS, TOK, 2 * D), vm(KHEADS, TOK, D), vm(KHEADS, TOK, D), vm(KHEADS, TOK, 2 * D),
            dma((4, KHEADS)), dma((4, KHEADS)),
            dma((NZ - 1, 2)), dma((NZ - 1, 2)), dma, dma,
            dma((NX - 1,)), dma((NX - 1,)), dma((NY - 1,)), dma((NY - 1,)),
            dma((NX - 1,)), dma((NX - 1,)), dma, dma,
            dma((NZ - 1, 2)), dma((NZ - 1, 2)),
        ],
        compiler_params=pltpu.CompilerParams(
            collective_id=0, has_side_effects=True, vmem_limit_bytes=VMEM_LIMIT),
        name="delta_layer",
    )(q, k, v, go, ld.reshape(KHEADS, 2, TOK), bl.reshape(KHEADS, 2, TOK))
    return (*outs, gd.reshape(HEADS, TOK), gb.reshape(HEADS, TOK))


def on_device(query_rows, key_rows, value_rows, log_decay, beta_logit, grad_out):
    return run_layer(query_rows, key_rows, value_rows, grad_out, log_decay, beta_logit)


def solution(mesh):
    rows = P(("ctx", "grp"), None)
    heads = P(None, ("ctx", "grp"))
    return jax.shard_map(
        on_device,
        mesh=mesh,
        in_specs=(rows, rows, rows, heads, heads, rows),
        out_specs=(rows, rows, rows, rows, heads, heads),
        check_vma=False,
    )
```

```python
import jax
import jax.numpy as jnp
from jax import lax
from jax.experimental import pallas as pl
from jax.experimental.pallas import tpu as pltpu
from jax.sharding import PartitionSpec as P

F32 = jnp.float32
BF16 = jnp.bfloat16
TOK = 256
D = 128
HEADS = 16
KHEADS = 8


def dg(a, b, ca, cb):
    return lax.dot_general(a, b, (((ca,), (cb,)), ((), ())), preferred_element_type=F32)


def split(x):
    hi = x.astype(BF16)
    return hi, (x - hi.astype(F32)).astype(BF16)


def halves(both):
    n = both.shape[1] // 2
    return both[:, :n] + both[:, n:]


def dot4(a, b, ca, cb):
    wide = jnp.concatenate(b, axis=1 - cb)
    return halves(dg(jnp.concatenate(a, axis=ca), jnp.concatenate([wide, wide], axis=cb), ca, cb))


def dot2r(a, b, ca, cb):
    return halves(dg(a, jnp.concatenate(b, axis=1 - cb), ca, cb))


def dot2l(a, b, ca, cb):
    return dg(a[0], b, ca, cb) + dg(a[1], b, ca, cb)


def dot3(a, b, ca, cb):
    return dot2r(a[0], b, ca, cb) + dg(a[1], b[0], ca, cb)


def iota(shape, dim):
    return lax.broadcasted_iota(jnp.int32, shape, dim)


def cumulate(rows, tri):
    hi = rows.astype(BF16)
    rest = rows - hi.astype(F32)
    mid = rest.astype(BF16)
    low = (rest - mid.astype(F32)).astype(BF16)
    parts = jnp.concatenate([hi.astype(F32), mid.astype(F32), low.astype(F32), jnp.zeros((2, TOK), F32)], axis=0)
    got = dg(parts.astype(BF16), tri, 1, 0)
    return got[0:2] + (got[2:4] + got[4:6])


def invert(systems):
    n = len(systems)
    lane = iota((16, D), 1)
    row = iota((16, D), 0)
    block = lane // 16
    packed = []
    for mat in systems:
        got = jnp.where(block == 0, mat[0:16], 0.0)
        for i in range(1, 8):
            got = jnp.where(block == i, mat[16 * i : 16 * i + 16], got)
        packed.append(got)
    inv = [jnp.where(lane % 16 == row, 1.0, 0.0).astype(F32) for _ in range(n)]
    for m in range(15):
        index = block * 16 + m
        for c in range(n):
            column = jnp.take_along_axis(packed[c], index, axis=1, mode="promise_in_bounds")
            inv[c] = inv[c] - column * inv[c][m : m + 1, :]
    wide_r = iota((D, D), 0)
    wide_c = iota((D, D), 1)
    full = [
        jnp.concatenate([jnp.where(block == i, inv[c], 0.0) for i in range(8)], axis=0)
        for c in range(n)
    ]
    for b in (16, 32, 64):
        mask = (wide_r // (2 * b) == wide_c // (2 * b)) & (wide_r // b % 2 == 1) & (wide_c // b % 2 == 0)
        sides = [split(jnp.where(mask, systems[c], 0.0)) for c in range(n)]
        ts = [split(full[c]) for c in range(n)]
        inner = [split(dot4(sides[c], ts[c], 1, 0)) for c in range(n)]
        full = [full[c] - dot4(ts[c], inner[c], 1, 0) for c in range(n)]
    return full


def rows_to_cols(rows8):
    return jnp.concatenate([rows8] * 16, axis=0).T


def cols_to_rows(cols):
    lane = iota((TOK, D), 1)
    got = jnp.zeros((TOK, D), F32)
    for i, col in enumerate(cols):
        got = jnp.where(lane == i, col, got)
    return got.T


VMEM_LIMIT = 60 * 1024 * 1024


def phase1(q_ref, k_ref, v_ref, go_ref, ld_ref, bl_ref,
           tri_ref, t_ref, m_ref, gam_ref, u_ref, w_ref, r_ref, aux_ref, end_ref):
    both = range(2)
    t_i = iota((TOK, TOK), 0)
    s_i = iota((TOK, TOK), 1)
    upper = jnp.where(t_i <= s_i, 1.0, 0.0).astype(BF16)
    within = t_i >= s_i
    q = [q_ref[:, j * D : (j + 1) * D] for j in both]
    k = [k_ref[:, j * D : (j + 1) * D] for j in both]
    kk = [dg(k[j], k[j], 1, 1) for j in both]
    qk = [dg(q[j], k[j], 1, 1) for j in both]
    run = cumulate(ld_ref[...], upper)
    beta_rows = 1.0 / (1.0 + jnp.exp(-bl_ref[...]))
    last = run[:, TOK - 1 : TOK]
    grown = jnp.exp(run)
    cols = rows_to_cols(jnp.concatenate([run, beta_rows, grown, jnp.exp(last - run)], axis=0))
    lane = iota((TOK, D), 1)
    kf = [part.astype(F32) for part in k]
    for j in both:
        for i, part in ((8, q[j].astype(F32)), (10, kf[j])):
            norm = lax.rsqrt(jnp.sum(part * part, axis=1, keepdims=True) + 1e-6)
            cols = jnp.where(lane == i + j, norm, cols)
    aux_ref[...] = cols
    norm_rows = cols.T
    rq = [cols[:, 8 + j : 9 + j] for j in both]
    rk = [cols[:, 10 + j : 11 + j] for j in both]
    g = [cols[:, 4 + j : 5 + j] for j in both]
    frk = [cols[:, 6 + j : 7 + j] * rk[j] for j in both]
    gam = [jnp.exp(jnp.where(within, cols[:, j : j + 1] - run[j : j + 1], -1e30)) * norm_rows[10 + j : 11 + j]
           for j in both]
    systems = [jnp.where(t_i > s_i, kk[j] * gam[j] * (cols[:, 2 + j : 3 + j] * rk[j]), 0.0) for j in both]
    blocks = []
    for j in both:
        blocks += [systems[j][:D, :D], systems[j][D:, D:]]
    mix = [split(qk[j] * gam[j] * rq[j]) for j in both]
    go_t = [go_ref[j].T for j in both]
    r_t = [dg(go_t[j], mix[j][0], 1, 0) + dg(go_t[j], mix[j][1], 1, 0) for j in both]
    for j in both:
        gam_ref[j] = gam[j]
        m_ref[j, 0] = mix[j][0]
        m_ref[j, 1] = mix[j][1]
        r_ref[j] = r_t[j]
    inv = [split(block) for block in invert(blocks)]
    inner = [split(dot4(split(systems[j][D:, :D]), inv[2 * j], 1, 0)) for j in both]
    t21 = [split(-dot4(inv[2 * j + 1], inner[j], 1, 0)) for j in both]
    tb = []
    for j in both:
        whole = []
        for i in range(2):
            t11, t22 = inv[2 * j][i], inv[2 * j + 1][i]
            whole.append(jnp.concatenate(
                [jnp.concatenate([t11, jnp.zeros((D, D), BF16)], axis=1),
                 jnp.concatenate([t21[j][i], t22], axis=1)], axis=0))
        tb.append(split((whole[0].astype(F32) + whole[1].astype(F32)) * beta_rows[j : j + 1]))
    ks = [split(kf[j] * (g[j] * rk[j])) for j in both]
    uw = [dot2l(tb[j], jnp.concatenate([v_ref[j], ks[j][0]], axis=1), 1, 0) for j in both]
    w = [uw[j][:, D:] + dg(tb[j][0], ks[j][1], 1, 0) for j in both]
    ws = [split(w[j]) for j in both]
    ends = [jnp.exp(last[j : j + 1]) for j in both]
    ab = [dot2r(k[j].T, split(jnp.concatenate([w[j] * frk[j], uw[j][:, :D] * frk[j]], axis=1)), 1, 0) for j in both]
    go_g = [split(go_t[j].astype(F32) * (grown[j : j + 1] * norm_rows[8 + j : 9 + j])) for j in both]
    offset = [dot2l(go_g[j], q[j], 1, 0) for j in both]
    offset = [offset[j] - dot3(split(r_t[j]), ws[j], 1, 0) for j in both]
    eye = jnp.where(iota((D, D), 0) == iota((D, D), 1), 1.0, 0.0)
    for j in both:
        tri_ref[j, 0] = eye * ends[j] - ab[j][:, :D]
        tri_ref[j, 1] = ab[j][:, D:].T
        tri_ref[j, 2] = offset[j]
        t_ref[j, 0] = tb[j][0]
        t_ref[j, 1] = tb[j][1]
        u_ref[j] = uw[j][:, :D]
        w_ref[j, 0] = ws[j][0]
        w_ref[j, 1] = ws[j][1]
        end_ref[j] = jnp.broadcast_to(ends[j], (8, D))


def phase3(part, q_ref, k_ref, v_ref, go_ref, bl_ref, sg_ref, t_ref, m_ref, gam_ref, u_ref, w_ref, r_ref, aux_ref,
           end_ref, out_ref, gq_ref, gk_ref, gv_ref, gd_ref, gb_ref):
    both = range(2)
    aux = aux_ref[...]
    aux_rows = aux.T
    frk_rows = aux_rows[6:8] * aux_rows[10:12]
    t_i = iota((TOK, TOK), 0)
    s_i = iota((TOK, TOK), 1)
    strict = t_i > s_i
    lower = jnp.where(t_i >= s_i, 1.0, 0.0).astype(BF16)
    q = [q_ref[:, j * D : (j + 1) * D] for j in both]
    k = [k_ref[:, j * D : (j + 1) * D] for j in both]
    v = [v_ref[j] for j in both]
    go = [go_ref[j] for j in both]
    rq = [aux[:, 8 + j : 9 + j] for j in both]
    rk = [aux[:, 10 + j : 11 + j] for j in both]
    g = [aux[:, 4 + j : 5 + j] for j in both]
    frk = [aux[:, 6 + j : 7 + j] * rk[j] for j in both]
    ss = [split(sg_ref[j, 0]) for j in both]
    gs = [split(sg_ref[j, 1]) for j in both]
    xw = [dot4((w_ref[j, 0], w_ref[j, 1]), ss[j], 1, 1) for j in both]
    kg = [dg(jnp.concatenate(gs[j], axis=0), k[j], 1, 1) for j in both]
    qs = [dot2r(q[j], ss[j], 1, 1) for j in both]
    gos = [dot2r(go[j], ss[j], 1, 0) for j in both]
    x = [u_ref[j] - xw[j] for j in both]
    xs = [split(x[j]) for j in both]
    dx_t = [split(r_ref[j] + (kg[j][:D] + kg[j][D:]) * frk_rows[j : j + 1]) for j in both]
    y_t = [dg(dx_t[j][0], t_ref[j, 0], 1, 0) + (dg(dx_t[j][0], t_ref[j, 1], 1, 0) + dg(dx_t[j][1], t_ref[j, 0], 1, 0))
           for j in both]
    gx = [dg(jnp.concatenate([go[j], go[j]], axis=1), jnp.concatenate(xs[j], axis=1), 1, 1) for j in both]
    y = [y_t[j].T for j in both]
    ys = [split(y[j]) for j in both]
    for j in both:
        gv_ref[j] = y[j]
    mx = [dot3((m_ref[j, 0], m_ref[j, 1]), xs[j], 1, 0) for j in both]
    n = [split(gx[j] * gam_ref[j] * rq[j]) for j in both]
    yx = [dg(jnp.concatenate(ys[j], axis=1), jnp.concatenate([xs[j][0], xs[j][0]], axis=1), 1, 1)
          + dg(ys[j][0], xs[j][1], 1, 1) for j in both]
    out = [qs[j] * (g[j] * rq[j]) + mx[j] for j in both]
    for j in both:
        out_ref[j] = out[j]
    k_t = [k[j].T for j in both]
    q_t = [q[j].T for j in both]
    xk = [dot2r(k_t[j], split(x[j] * frk[j]), 1, 0) for j in both]
    ends = [jnp.sum(sg_ref[j, 1] * (sg_ref[j, 0] * end_ref[j][0:1] + xk[j].T), keepdims=True) for j in both]
    turned = [dg(q_t[j], n[j][0], 1, 0) + dg(q_t[j], n[j][1], 1, 0) for j in both]
    eq = [dot2l(n[j], k[j], 1, 0) for j in both]
    p = [split(jnp.where(strict, yx[j] * gam_ref[j] * (-rk[j]), 0.0)) for j in both]
    turned = [turned[j] + (dg(k_t[j], p[j][0], 1, 0) + dg(k_t[j], p[j][1], 1, 0)) for j in both]
    ek = [dot2l(p[j], k[j], 1, 0) for j in both]
    xg = [dot4(xs[j], gs[j], 1, 0) for j in both]
    sy = [dot4(ys[j], ss[j], 1, 0) for j in both]
    eq = [eq[j] + gos[j] * (g[j] * rq[j]) for j in both]
    ek = [ek[j] + turned[j].T + (xg[j] * frk[j] - sy[j] * (g[j] * rk[j])) for j in both]
    dots = [jnp.sum(go[j].astype(F32) * out[j] - v[j].astype(F32) * y[j], axis=1, keepdims=True) for j in both]
    dots += [jnp.sum(y[j] * x[j], axis=1, keepdims=True) for j in both]

    @pl.when(part == 0)
    def _():
        for j in both:
            gq_ref[:, j * D : (j + 1) * D] = eq[j]
            gk_ref[:, j * D : (j + 1) * D] = ek[j]

    @pl.when(part == 1)
    def _():
        for j in both:
            cols = slice(j * D, (j + 1) * D)
            for raw, ref, row, norm in ((q[j], gq_ref, eq[j], rq[j]), (k[j], gk_ref, ek[j], rk[j])):
                row = row + ref[:, cols]
                raw = raw.astype(F32)
                ref[:, cols] = row - raw * (norm * norm * jnp.sum(raw * row, axis=1, keepdims=True))

    rows = cols_to_rows(dots)
    suffix = cumulate(rows[0:2], lower)
    gd_ref[...] = suffix + jnp.concatenate(ends, axis=0)
    gb_ref[...] = jnp.exp(-bl_ref[...]) * rows[2:4]


MESH = pl.DeviceIdType.MESH
NZ, NC, NX, NY = 4, 2, 4, 4
SHARE = HEADS // NZ
PARTS = 2
QUARTER = D // NX


def join(early, late):
    ae, be, ce = early
    al, bl, cl = late
    als = split(al)
    cls = split(cl)
    left = (jnp.concatenate([als[0], cls[0]], axis=0), jnp.concatenate([als[1], cls[1]], axis=0))
    both = dot4(left, split(ae), 1, 0)
    return both[:D], dot4(split(be), als, 1, 1) + bl, both[D:] + ce


def join_all(parts):
    while len(parts) > 1:
        parts = [join(parts[i], parts[i + 1]) for i in range(0, len(parts), 2)]
    return parts[0]


def chain(parts, state, grad):
    split_a = [split(p[0]) for p in parts]
    states = [state]
    for i in range(len(parts) - 1):
        states.append(dot4(split(states[-1]), split_a[i], 1, 1) + parts[i][1])
    grads = [grad]
    for i in range(len(parts) - 1, 0, -1):
        grads.append(dot4(split(grads[-1]), split_a[i], 1, 0) + parts[i][2])
    return states, grads[::-1]


def place(i):
    r = lax.rem(i, NZ)
    return lax.rem(lax.div(3 * r * r + 4 - 5 * r, 2), NZ), lax.div(i, NZ)


def layer_kernel(q_hbm, k_hbm, v_hbm, go_hbm, ld_ref, bl_ref,
                 out_hbm, gq_hbm, gk_hbm, gv_hbm, gd_ref, gb_ref,
                 qb, kb, vb, gob, ldp, blp, gdp, gbp, t_ref, m_ref, gam_ref, u_ref, w_ref, r_ref, aux_ref, end_ref,
                 tri, zin, cout, cin, xout, xin, yin, xdo, xdi, cdo, cdi, zdo, sgin,
                 outb, gqb, gkb, gvb,
                 ins, outs, zs, zr, cs, cr, xs, xr, ys, yr, xds, xdr, cds, cdr, zds, zdr):
    ctx = lax.axis_index("ctx")
    z = lax.axis_index("grp")
    c = lax.rem(ctx, NC)
    x = lax.rem(lax.div(ctx, NC), NX)
    y = lax.div(ctx, NC * NX)
    oc = 1 - c

    def at(yy, xx, cc, zz):
        return ((yy * NX + xx) * NC + cc, zz)

    def zpeer(d):
        return lax.rem(z + d, NZ)

    def xpeer(d):
        return lax.rem(x + d, NX)

    def ypeer(d):
        return lax.rem(y + d, NY)

    barrier = pltpu.get_barrier_semaphore()
    peers = [at(y, x, c, zpeer(d)) for d in range(1, NZ)]
    peers += [at(y, x, oc, z)]
    peers += [at(y, xpeer(d), c, z) for d in range(1, NX)]
    peers += [at(ypeer(d), x, c, z) for d in range(1, NY)]
    for peer in peers:
        pl.semaphore_signal(barrier, inc=1, device_id=peer, device_id_type=MESH)

    def lanes(head, width):
        return pl.ds(pl.multiple_of(head * width, width), width)

    def rows_of(zz):
        both = lanes(zz, 2 * D)
        return [pltpu.make_async_copy(q_hbm.at[:, both], qb.at[zz], ins.at[0, zz]),
                pltpu.make_async_copy(k_hbm.at[:, both], kb.at[zz], ins.at[1, zz])]

    def values_of(zz, part):
        copies = []
        for j in range(2):
            one = lanes(SHARE * zz + 2 * j + part, D)
            slot = 2 * zz + part
            copies.append(pltpu.make_async_copy(v_hbm.at[:, one], vb.at[slot, j], ins.at[2 + j, slot]))
            copies.append(pltpu.make_async_copy(go_hbm.at[:, one], gob.at[slot, j], ins.at[4 + j, slot]))
        return copies

    def outputs_of(zz, part):
        copies = []
        for j in range(2):
            one = lanes(SHARE * zz + 2 * j + part, D)
            slot = 2 * zz + part
            copies.append(pltpu.make_async_copy(outb.at[slot, j], out_hbm.at[:, one], outs.at[2 + j, slot]))
            copies.append(pltpu.make_async_copy(gvb.at[slot, j], gv_hbm.at[:, one], outs.at[4 + j, slot]))
        return copies

    def grads_of(zz):
        both = lanes(zz, 2 * D)
        return [pltpu.make_async_copy(gqb.at[zz], gq_hbm.at[:, both], outs.at[0, zz]),
                pltpu.make_async_copy(gkb.at[zz], gk_hbm.at[:, both], outs.at[1, zz])]

    def load_start(i, _):
        d, part = place(i)
        zz = zpeer(d)

        @pl.when(part == 0)
        def _():
            for copy in rows_of(zz):
                copy.start()

        for copy in values_of(zz, part):
            copy.start()
        return 0

    lax.fori_loop(0, NZ * PARTS, load_start, 0)
    for zz in range(NZ):
        for part in range(PARTS):
            for j in range(2):
                h = SHARE * zz + 2 * j + part
                ldp[2 * zz + part, j : j + 1] = ld_ref[h : h + 1]
                blp[2 * zz + part, j : j + 1] = bl_ref[h : h + 1]

    def remote(src, dst, send, recv, peer):
        return pltpu.make_async_remote_copy(
            src_ref=src, dst_ref=dst, send_sem=send, recv_sem=recv, device_id=peer, device_id_type=MESH)

    def zcopy(d, part):
        to = zpeer(d)
        return remote(tri.at[2 * to + part], zin.at[part, z], zs.at[d - 1, part], zr.at[d - 1, part], at(y, x, c, to))

    def ccopy(part):
        return remote(cout.at[part], cin.at[part, c], cs.at[part], cr.at[part], at(y, x, oc, z))

    def xcopy(d, part):
        return remote(xout.at[part, xpeer(d)], xin.at[part, x], xs.at[d - 1, part], xr.at[d - 1, part],
                      at(y, xpeer(d), c, z))

    def ycopy(d, part):
        return remote(yin.at[part, y], yin.at[part, y], ys.at[d - 1, part], yr.at[d - 1, part],
                      at(ypeer(d), x, c, z))

    def xdcopy(d, part):
        return remote(xdo.at[part, xpeer(d)], xdi.at[part, x], xds.at[d - 1, part], xdr.at[d - 1, part],
                      at(y, xpeer(d), c, z))

    def cdcopy(part):
        return remote(cdo.at[part, oc], cdi.at[part], cds.at[part], cdr.at[part], at(y, x, oc, z))

    def zdcopy(d, part, half):
        to = zpeer(d)
        core = lax.rem(c + half, NC)
        pair = NC * part + half
        return remote(zdo.at[part, to, core], sgin.at[part, z, core], zds.at[d - 1, pair], zdr.at[d - 1, pair],
                      at(y, x, c, to))

    def triple(ref):
        return ref[0], ref[1], ref[2]

    def packed(ref):
        return ref[0:D], ref[D : D + QUARTER], ref[D + QUARTER : D + 2 * QUARTER]

    def join_z(part):
        zin[part, z] = tri[2 * z + part]
        for d in range(1, NZ):
            zcopy(d, part).wait_recv()
        got = join_all([triple(zin.at[part, m, oc]) for m in range(NZ)])
        for i in range(3):
            cout[part, i] = got[i]
        ccopy(part).start()
        got = join_all([triple(zin.at[part, m, c]) for m in range(NZ)])
        for i in range(3):
            cin[part, c, i] = got[i]

    def join_core(part):
        ccopy(part).wait_recv()
        a, b, g = join_all([triple(cin.at[part, m]) for m in range(NC)])
        for to in range(NX):
            rows = slice(to * QUARTER, (to + 1) * QUARTER)
            xout[part, to, 0:D] = a
            xout[part, to, D : D + QUARTER] = b[rows]
            xout[part, to, D + QUARTER : D + 2 * QUARTER] = g[rows]
        for d in (2, 1, 3):
            xcopy(d, part).start()
        xin[part, x] = xout[part, x]

    def join_x(part):
        for d in range(1, NX):
            xcopy(d, part).wait_recv()
        row = join_all([packed(xin.at[part, m]) for m in range(NX)])
        yin[part, y, 0:D] = row[0]
        yin[part, y, D : D + QUARTER] = row[1]
        yin[part, y, D + QUARTER : D + 2 * QUARTER] = row[2]
        for d in (2, 1, 3):
            ycopy(d, part).start()

    def down_x(part):
        for d in range(1, NY):
            ycopy(d, part).wait_recv()
        zero = jnp.zeros((QUARTER, D), F32)
        states, grads = chain([packed(yin.at[part, m]) for m in range(NY)], zero, zero)
        state, grad = states[0], grads[0]
        for m in range(1, NY):
            state = jnp.where(y == m, states[m], state)
            grad = jnp.where(y == m, grads[m], grad)
        states, grads = chain([packed(xin.at[part, m]) for m in range(NX)], state, grad)
        for m in range(NX):
            xdo[part, m, 0:QUARTER] = states[m]
            xdo[part, m, QUARTER : 2 * QUARTER] = grads[m]
        for d in (2, 1, 3):
            xdcopy(d, part).start()
        xdi[part, x] = xdo[part, x]

    def down_core(part):
        for d in range(1, NX):
            xdcopy(d, part).wait_recv()
        state = jnp.concatenate([xdi[part, m, 0:QUARTER] for m in range(NX)], axis=0)
        grad = jnp.concatenate([xdi[part, m, QUARTER : 2 * QUARTER] for m in range(NX)], axis=0)
        states, grads = chain([triple(cin.at[part, m]) for m in range(NC)], state, grad)
        for m in range(NC):
            cdo[part, m, 0] = states[m]
            cdo[part, m, 1] = grads[m]
        cdcopy(part).start()

    def down_z(part):
        def one(core, state, grad):
            states, grads = chain([triple(zin.at[part, m, core]) for m in range(NZ)], state, grad)
            for m in range(NZ):
                zdo[part, m, core, 0] = states[m]
                zdo[part, m, core, 1] = grads[m]

        one(c, cdo[part, c, 0], cdo[part, c, 1])
        for d in (2, 1, 3):
            zdcopy(d, part, 0).start()
        cdcopy(part).wait_recv()
        one(oc, cdi[part, 0], cdi[part, 1])
        for d in (2, 1, 3):
            zdcopy(d, part, 1).start()
        sgin[part, z] = zdo[part, z]

    pl.semaphore_wait(barrier, len(peers))

    def up(i, _):
        d, part = place(i)
        zz = zpeer(d)
        slot = 2 * zz + part

        @pl.when(part == 0)
        def _():
            for copy in rows_of(zz):
                copy.wait()

        for copy in values_of(zz, part):
            copy.wait()
        phase1(qb.at[zz], kb.at[zz], vb.at[slot], gob.at[slot], ldp.at[slot], blp.at[slot], tri.at[slot],
               t_ref.at[slot], m_ref.at[slot], gam_ref.at[slot], u_ref.at[slot], w_ref.at[slot], r_ref.at[slot],
               aux_ref.at[slot], end_ref.at[slot])

        @pl.when(lax.rem(i, NZ) < NZ - 1)
        def _():
            zcopy(d, part).start()

        for step, stage in UP_STAGES:
            @pl.when(i == step)
            def _():
                stage_of[stage](0)

        return 0

    stage_of = dict(z=join_z, core=join_core, x=join_x, dx=down_x, dcore=down_core, dz=down_z)
    lax.fori_loop(0, NZ * PARTS, up, 0)
    for stage, part in MIDDLE:
        stage_of[stage](part)

    def down(i, _):
        d, part = place(lax.rem(i, NZ) + NZ - 1)
        part = lax.div(i, NZ)
        for step, stage in DOWN_STAGES:
            @pl.when(i == step)
            def _():
                stage_of[stage](1)

        @pl.when(lax.rem(i, NZ) > 0)
        def _():
            zdcopy(d, part, 0).wait_recv()
            zdcopy(d, part, 1).wait_recv()

        zz = lax.rem(z + NZ - d, NZ)
        slot = 2 * zz + part
        phase3(part, qb.at[zz], kb.at[zz], vb.at[slot], gob.at[slot], blp.at[slot], sgin.at[part, zz],
               t_ref.at[slot], m_ref.at[slot], gam_ref.at[slot], u_ref.at[slot], w_ref.at[slot], r_ref.at[slot],
               aux_ref.at[slot], end_ref.at[slot],
               outb.at[slot], gqb.at[zz], gkb.at[zz], gvb.at[slot], gdp.at[slot], gbp.at[slot])
        for copy in outputs_of(zz, part):
            copy.start()

        @pl.when(part == PARTS - 1)
        def _():
            for copy in grads_of(zz):
                copy.start()

        return 0

    lax.fori_loop(0, NZ * PARTS, down, 0)
    for zz in range(NZ):
        for part in range(PARTS):
            for j in range(2):
                h = SHARE * zz + 2 * j + part
                gd_ref[h : h + 1] = gdp[2 * zz + part, j : j + 1]
                gb_ref[h : h + 1] = gbp[2 * zz + part, j : j + 1]

    for part in range(PARTS):
        for d in range(1, NZ):
            zcopy(d, part).wait_send()
            zdcopy(d, part, 0).wait_send()
            zdcopy(d, part, 1).wait_send()
            xcopy(d, part).wait_send()
            xdcopy(d, part).wait_send()
            ycopy(d, part).wait_send()
        ccopy(part).wait_send()
        cdcopy(part).wait_send()

    def store_wait(zz, _):
        for copy in grads_of(zz):
            copy.wait()
        for part in range(PARTS):
            for copy in outputs_of(zz, part):
                copy.wait()
        return 0

    lax.fori_loop(0, NZ, store_wait, 0)


UP_STAGES = ((5, "z"), (6, "core"), (7, "x"))
MIDDLE = (("dx", 0), ("z", 1), ("core", 1), ("dcore", 0), ("dz", 0), ("x", 1))
DOWN_STAGES = ((1, "dx"), (2, "dcore"), (2, "dz"))


def run_layer(q, k, v, go, ld, bl):
    dma = pltpu.SemaphoreType.DMA

    def vm(*shape, dtype=F32):
        return pltpu.VMEM(shape, dtype)

    hbm = pl.BlockSpec(memory_space=pl.ANY)
    vmem = pl.BlockSpec(memory_space=pltpu.VMEM)
    slots = NZ * PARTS
    piece = D + 2 * QUARTER
    return pl.pallas_call(
        layer_kernel,
        in_specs=[hbm] * 4 + [vmem] * 2,
        out_specs=[hbm] * 4 + [vmem] * 2,
        out_shape=[
            jax.ShapeDtypeStruct((TOK, HEADS * D), F32),
            jax.ShapeDtypeStruct((TOK, KHEADS * D), F32),
            jax.ShapeDtypeStruct((TOK, KHEADS * D), F32),
            jax.ShapeDtypeStruct((TOK, HEADS * D), F32),
            jax.ShapeDtypeStruct((HEADS, TOK), F32),
            jax.ShapeDtypeStruct((HEADS, TOK), F32),
        ],
        scratch_shapes=[
            vm(NZ, TOK, 2 * D, dtype=BF16), vm(NZ, TOK, 2 * D, dtype=BF16),
            vm(slots, 2, TOK, D, dtype=BF16), vm(slots, 2, TOK, D, dtype=BF16),
            vm(slots, 2, TOK), vm(slots, 2, TOK), vm(slots, 2, TOK), vm(slots, 2, TOK),
            vm(slots, 2, 2, TOK, TOK, dtype=BF16), vm(slots, 2, 2, TOK, TOK, dtype=BF16), vm(slots, 2, TOK, TOK),
            vm(slots, 2, TOK, D), vm(slots, 2, 2, TOK, D, dtype=BF16), vm(slots, 2, D, TOK),
            vm(slots, TOK, D), vm(slots, 2, 8, D),
            vm(slots, NC, 3, D, D), vm(PARTS, NZ, NC, 3, D, D),
            vm(PARTS, 3, D, D), vm(PARTS, NC, 3, D, D),
            vm(PARTS, NX, piece, D), vm(PARTS, NX, piece, D), vm(PARTS, NY, piece, D),
            vm(PARTS, NX, 2 * QUARTER, D), vm(PARTS, NX, 2 * QUARTER, D),
            vm(PARTS, NC, 2, D, D), vm(PARTS, 2, D, D),
            vm(PARTS, NZ, NC, 2, D, D), vm(PARTS, NZ, NC, 2, D, D),
            vm(slots, 2, TOK, D), vm(NZ, TOK, 2 * D), vm(NZ, TOK, 2 * D), vm(slots, 2, TOK, D),
            dma((6, slots)), dma((6, slots)),
            dma((NZ - 1, PARTS)), dma((NZ - 1, PARTS)), dma((PARTS,)), dma((PARTS,)),
            dma((NX - 1, PARTS)), dma((NX - 1, PARTS)), dma((NY - 1, PARTS)), dma((NY - 1, PARTS)),
            dma((NX - 1, PARTS)), dma((NX - 1, PARTS)), dma((PARTS,)), dma((PARTS,)),
            dma((NZ - 1, NC * PARTS)), dma((NZ - 1, NC * PARTS)),
        ],
        compiler_params=pltpu.CompilerParams(
            collective_id=0, has_side_effects=True, vmem_limit_bytes=VMEM_LIMIT),
        name="delta_layer",
    )(q, k, v, go, ld, bl)


def on_device(query_rows, key_rows, value_rows, log_decay, beta_logit, grad_out):
    return tuple(run_layer(query_rows, key_rows, value_rows, grad_out, log_decay, beta_logit))


def solution(mesh):
    rows = P(("ctx", "grp"), None)
    heads = P(None, ("ctx", "grp"))
    return jax.shard_map(
        on_device,
        mesh=mesh,
        in_specs=(rows, rows, rows, heads, heads, rows),
        out_specs=(rows, rows, rows, rows, heads, heads),
        check_vma=False,
    )
```

```python
import jax
import jax.numpy as jnp
from jax import lax
from jax.experimental import pallas as pl
from jax.experimental.pallas import tpu as pltpu
from jax.sharding import PartitionSpec as P

F32 = jnp.float32
BF16 = jnp.bfloat16
TOK = 256
D = 128
HEADS = 16
KHEADS = 8


def dg(a, b, ca, cb):
    return lax.dot_general(a, b, (((ca,), (cb,)), ((), ())), preferred_element_type=F32)


def split(x):
    hi = x.astype(BF16)
    return hi, (x - hi.astype(F32)).astype(BF16)


def halves(both):
    n = both.shape[1] // 2
    return both[:, :n] + both[:, n:]


def dot4(a, b, ca, cb):
    wide = jnp.concatenate(b, axis=1 - cb)
    return halves(dg(jnp.concatenate(a, axis=ca), jnp.concatenate([wide, wide], axis=cb), ca, cb))


def dot2r(a, b, ca, cb):
    return halves(dg(a, jnp.concatenate(b, axis=1 - cb), ca, cb))


def dot2l(a, b, ca, cb):
    return dg(a[0], b, ca, cb) + dg(a[1], b, ca, cb)


def dot3(a, b, ca, cb):
    return dot2r(a[0], b, ca, cb) + dg(a[1], b[0], ca, cb)


def iota(shape, dim):
    return lax.broadcasted_iota(jnp.int32, shape, dim)


def cumulate(rows, tri):
    hi = rows.astype(BF16)
    rest = rows - hi.astype(F32)
    mid = rest.astype(BF16)
    low = (rest - mid.astype(F32)).astype(BF16)
    parts = jnp.concatenate([hi.astype(F32), mid.astype(F32), low.astype(F32), jnp.zeros((2, TOK), F32)], axis=0)
    got = dg(parts.astype(BF16), tri, 1, 0)
    return got[0:2] + (got[2:4] + got[4:6])


def invert(systems):
    n = len(systems)
    lane = iota((16, D), 1)
    row = iota((16, D), 0)
    block = lane // 16
    packed = []
    for mat in systems:
        got = jnp.where(block == 0, mat[0:16], 0.0)
        for i in range(1, 8):
            got = jnp.where(block == i, mat[16 * i : 16 * i + 16], got)
        packed.append(got)
    inv = [jnp.where(lane % 16 == row, 1.0, 0.0).astype(F32) for _ in range(n)]
    for m in range(15):
        index = block * 16 + m
        for c in range(n):
            column = jnp.take_along_axis(packed[c], index, axis=1, mode="promise_in_bounds")
            inv[c] = inv[c] - column * inv[c][m : m + 1, :]
    wide_r = iota((D, D), 0)
    wide_c = iota((D, D), 1)
    full = [
        jnp.concatenate([jnp.where(block == i, inv[c], 0.0) for i in range(8)], axis=0)
        for c in range(n)
    ]
    for b in (16, 32, 64):
        mask = (wide_r // (2 * b) == wide_c // (2 * b)) & (wide_r // b % 2 == 1) & (wide_c // b % 2 == 0)
        sides = [split(jnp.where(mask, systems[c], 0.0)) for c in range(n)]
        ts = [split(full[c]) for c in range(n)]
        inner = [split(dot4(sides[c], ts[c], 1, 0)) for c in range(n)]
        full = [full[c] - dot4(ts[c], inner[c], 1, 0) for c in range(n)]
    return full


def rows_to_cols(rows8):
    return jnp.concatenate([rows8] * 16, axis=0).T


def cols_to_rows(cols):
    lane = iota((TOK, D), 1)
    got = jnp.zeros((TOK, D), F32)
    for i, col in enumerate(cols):
        got = jnp.where(lane == i, col, got)
    return got.T


VMEM_LIMIT = 60 * 1024 * 1024


def phase1(q_ref, k_ref, v_ref, go_ref, ld_ref, bl_ref,
           tri_ref, t_ref, m_ref, gam_ref, u_ref, w_ref, r_ref, aux_ref, end_ref):
    both = range(2)
    t_i = iota((TOK, TOK), 0)
    s_i = iota((TOK, TOK), 1)
    upper = jnp.where(t_i <= s_i, 1.0, 0.0).astype(BF16)
    within = t_i >= s_i
    q = [q_ref[:, j * D : (j + 1) * D] for j in both]
    k = [k_ref[:, j * D : (j + 1) * D] for j in both]
    kk = [dg(k[j], k[j], 1, 1) for j in both]
    qk = [dg(q[j], k[j], 1, 1) for j in both]
    run = cumulate(ld_ref[...], upper)
    beta_rows = 1.0 / (1.0 + jnp.exp(-bl_ref[...]))
    last = run[:, TOK - 1 : TOK]
    grown = jnp.exp(run)
    cols = rows_to_cols(jnp.concatenate([run, beta_rows, grown, jnp.exp(last - run)], axis=0))
    lane = iota((TOK, D), 1)
    kf = [part.astype(F32) for part in k]
    for j in both:
        for i, part in ((8, q[j].astype(F32)), (10, kf[j])):
            norm = lax.rsqrt(jnp.sum(part * part, axis=1, keepdims=True) + 1e-6)
            cols = jnp.where(lane == i + j, norm, cols)
    aux_ref[...] = cols
    norm_rows = cols.T
    rq = [cols[:, 8 + j : 9 + j] for j in both]
    rk = [cols[:, 10 + j : 11 + j] for j in both]
    g = [cols[:, 4 + j : 5 + j] for j in both]
    frk = [cols[:, 6 + j : 7 + j] * rk[j] for j in both]
    gam = [jnp.exp(jnp.where(within, cols[:, j : j + 1] - run[j : j + 1], -1e30)) * norm_rows[10 + j : 11 + j]
           for j in both]
    systems = [jnp.where(t_i > s_i, kk[j] * gam[j] * (cols[:, 2 + j : 3 + j] * rk[j]), 0.0) for j in both]
    blocks = []
    for j in both:
        blocks += [systems[j][:D, :D], systems[j][D:, D:]]
    mix = [split(qk[j] * gam[j] * rq[j]) for j in both]
    go_t = [go_ref[j].T for j in both]
    r_t = [dg(go_t[j], mix[j][0], 1, 0) + dg(go_t[j], mix[j][1], 1, 0) for j in both]
    for j in both:
        gam_ref[j] = gam[j]
        m_ref[j, 0] = mix[j][0]
        m_ref[j, 1] = mix[j][1]
        r_ref[j] = r_t[j]
    inv = [split(block) for block in invert(blocks)]
    inner = [split(dot4(split(systems[j][D:, :D]), inv[2 * j], 1, 0)) for j in both]
    t21 = [split(-dot4(inv[2 * j + 1], inner[j], 1, 0)) for j in both]
    tb = []
    for j in both:
        whole = []
        for i in range(2):
            t11, t22 = inv[2 * j][i], inv[2 * j + 1][i]
            whole.append(jnp.concatenate(
                [jnp.concatenate([t11, jnp.zeros((D, D), BF16)], axis=1),
                 jnp.concatenate([t21[j][i], t22], axis=1)], axis=0))
        tb.append(split((whole[0].astype(F32) + whole[1].astype(F32)) * beta_rows[j : j + 1]))
    ks = [split(kf[j] * (g[j] * rk[j])) for j in both]
    uw = [dot2l(tb[j], jnp.concatenate([v_ref[j], ks[j][0]], axis=1), 1, 0) for j in both]
    w = [uw[j][:, D:] + dg(tb[j][0], ks[j][1], 1, 0) for j in both]
    ws = [split(w[j]) for j in both]
    ends = [jnp.exp(last[j : j + 1]) for j in both]
    ab = [dot2r(k[j].T, split(jnp.concatenate([w[j] * frk[j], uw[j][:, :D] * frk[j]], axis=1)), 1, 0) for j in both]
    go_g = [split(go_t[j].astype(F32) * (grown[j : j + 1] * norm_rows[8 + j : 9 + j])) for j in both]
    offset = [dot2l(go_g[j], q[j], 1, 0) for j in both]
    offset = [offset[j] - dot3(split(r_t[j]), ws[j], 1, 0) for j in both]
    eye = jnp.where(iota((D, D), 0) == iota((D, D), 1), 1.0, 0.0)
    for j in both:
        tri_ref[j, 0] = eye * ends[j] - ab[j][:, :D]
        tri_ref[j, 1] = ab[j][:, D:].T
        tri_ref[j, 2] = offset[j]
        t_ref[j, 0] = tb[j][0]
        t_ref[j, 1] = tb[j][1]
        u_ref[j] = uw[j][:, :D]
        w_ref[j, 0] = ws[j][0]
        w_ref[j, 1] = ws[j][1]
        end_ref[j] = jnp.broadcast_to(ends[j], (8, D))


def phase3(part, q_ref, k_ref, v_ref, go_ref, bl_ref, sg_ref, t_ref, m_ref, gam_ref, u_ref, w_ref, r_ref, aux_ref,
           end_ref, out_ref, gq_ref, gk_ref, gv_ref, gd_ref, gb_ref):
    both = range(2)
    aux = aux_ref[...]
    aux_rows = aux.T
    frk_rows = aux_rows[6:8] * aux_rows[10:12]
    t_i = iota((TOK, TOK), 0)
    s_i = iota((TOK, TOK), 1)
    strict = t_i > s_i
    lower = jnp.where(t_i >= s_i, 1.0, 0.0).astype(BF16)
    q = [q_ref[:, j * D : (j + 1) * D] for j in both]
    k = [k_ref[:, j * D : (j + 1) * D] for j in both]
    v = [v_ref[j] for j in both]
    go = [go_ref[j] for j in both]
    rq = [aux[:, 8 + j : 9 + j] for j in both]
    rk = [aux[:, 10 + j : 11 + j] for j in both]
    g = [aux[:, 4 + j : 5 + j] for j in both]
    frk = [aux[:, 6 + j : 7 + j] * rk[j] for j in both]
    ss = [split(sg_ref[j, 0]) for j in both]
    gs = [split(sg_ref[j, 1]) for j in both]
    xw = [dot4((w_ref[j, 0], w_ref[j, 1]), ss[j], 1, 1) for j in both]
    kg = [dg(jnp.concatenate(gs[j], axis=0), k[j], 1, 1) for j in both]
    qs = [dot2r(q[j], ss[j], 1, 1) for j in both]
    gos = [dot2r(go[j], ss[j], 1, 0) for j in both]
    x = [u_ref[j] - xw[j] for j in both]
    xs = [split(x[j]) for j in both]
    dx_t = [split(r_ref[j] + (kg[j][:D] + kg[j][D:]) * frk_rows[j : j + 1]) for j in both]
    y_t = [dg(dx_t[j][0], t_ref[j, 0], 1, 0) + (dg(dx_t[j][0], t_ref[j, 1], 1, 0) + dg(dx_t[j][1], t_ref[j, 0], 1, 0))
           for j in both]
    gx = [dg(jnp.concatenate([go[j], go[j]], axis=1), jnp.concatenate(xs[j], axis=1), 1, 1) for j in both]
    y = [y_t[j].T for j in both]
    ys = [split(y[j]) for j in both]
    for j in both:
        gv_ref[j] = y[j]
    mx = [dot3((m_ref[j, 0], m_ref[j, 1]), xs[j], 1, 0) for j in both]
    n = [split(gx[j] * gam_ref[j] * rq[j]) for j in both]
    yx = [dg(jnp.concatenate(ys[j], axis=1), jnp.concatenate([xs[j][0], xs[j][0]], axis=1), 1, 1)
          + dg(ys[j][0], xs[j][1], 1, 1) for j in both]
    out = [qs[j] * (g[j] * rq[j]) + mx[j] for j in both]
    for j in both:
        out_ref[j] = out[j]
    k_t = [k[j].T for j in both]
    q_t = [q[j].T for j in both]
    xk = [dot2r(k_t[j], split(x[j] * frk[j]), 1, 0) for j in both]
    ends = [jnp.sum(sg_ref[j, 1] * (sg_ref[j, 0] * end_ref[j][0:1] + xk[j].T), keepdims=True) for j in both]
    turned = [dg(q_t[j], n[j][0], 1, 0) + dg(q_t[j], n[j][1], 1, 0) for j in both]
    eq = [dot2l(n[j], k[j], 1, 0) for j in both]
    p = [split(jnp.where(strict, yx[j] * gam_ref[j] * (-rk[j]), 0.0)) for j in both]
    turned = [turned[j] + (dg(k_t[j], p[j][0], 1, 0) + dg(k_t[j], p[j][1], 1, 0)) for j in both]
    ek = [dot2l(p[j], k[j], 1, 0) for j in both]
    xg = [dot4(xs[j], gs[j], 1, 0) for j in both]
    sy = [dot4(ys[j], ss[j], 1, 0) for j in both]
    eq = [eq[j] + gos[j] * (g[j] * rq[j]) for j in both]
    ek = [ek[j] + turned[j].T + (xg[j] * frk[j] - sy[j] * (g[j] * rk[j])) for j in both]
    dots = [jnp.sum(go[j].astype(F32) * out[j] - v[j].astype(F32) * y[j], axis=1, keepdims=True) for j in both]
    dots += [jnp.sum(y[j] * x[j], axis=1, keepdims=True) for j in both]

    @pl.when(part == 0)
    def _():
        for j in both:
            gq_ref[:, j * D : (j + 1) * D] = eq[j]
            gk_ref[:, j * D : (j + 1) * D] = ek[j]

    @pl.when(part == 1)
    def _():
        for j in both:
            cols = slice(j * D, (j + 1) * D)
            for raw, ref, row, norm in ((q[j], gq_ref, eq[j], rq[j]), (k[j], gk_ref, ek[j], rk[j])):
                row = row + ref[:, cols]
                raw = raw.astype(F32)
                ref[:, cols] = row - raw * (norm * norm * jnp.sum(raw * row, axis=1, keepdims=True))

    rows = cols_to_rows(dots)
    suffix = cumulate(rows[0:2], lower)
    gd_ref[...] = suffix + jnp.concatenate(ends, axis=0)
    gb_ref[...] = jnp.exp(-bl_ref[...]) * rows[2:4]


MESH = pl.DeviceIdType.MESH
NZ, NC, NX, NY = 4, 2, 4, 4
SHARE = HEADS // NZ
PARTS = 2
QUARTER = D // NX


def join_all(parts):
    while len(parts) > 1:
        early, late = parts[0::2], parts[1::2]
        n = range(len(early))
        late_a = [split(p[0]) for p in late]
        late_c = [split(p[2]) for p in late]
        early_a = [split(p[0]) for p in early]
        early_b = [split(p[1]) for p in early]
        left = [[jnp.concatenate([a, g], axis=0) for a, g in zip(late_a[i], late_c[i])] for i in n]
        down = [dot4(left[i], early_a[i], 1, 0) for i in n]
        up = [dot4(early_b[i], late_a[i], 1, 1) for i in n]
        parts = [(down[i][:D], up[i] + late[i][1], down[i][D:] + early[i][2]) for i in n]
    return parts[0]


def chain(parts, state, grad):
    split_a = [split(p[0]) for p in parts]
    n = len(parts)
    states = [state]
    grads = [grad]
    for i in range(n - 1):
        ss, gs = split(states[-1]), split(grads[-1])
        moved = dot4(ss, split_a[i], 1, 1)
        back = dot4(gs, split_a[n - 1 - i], 1, 0)
        states.append(moved + parts[i][1])
        grads.append(back + parts[n - 1 - i][2])
    return states, grads[::-1]


def place(i):
    r = lax.rem(i, NZ)
    return lax.rem(lax.div(3 * r * r + 4 - 5 * r, 2), NZ), lax.div(i, NZ)


def layer_kernel(q_hbm, k_hbm, v_hbm, go_hbm, ld_ref, bl_ref,
                 out_hbm, gq_hbm, gk_hbm, gv_hbm, gd_ref, gb_ref,
                 qb, kb, vb, gob, ldp, blp, gdp, gbp, t_ref, m_ref, gam_ref, u_ref, w_ref, r_ref, aux_ref, end_ref,
                 tri, zin, cout, cin, xout, xin, yin, xdo, xdi, cdo, cdi, zdo, sgin,
                 outb, gqb, gkb, gvb,
                 ins, outs, zs, zr, cs, cr, xs, xr, ys, yr, xds, xdr, cds, cdr, zds, zdr):
    ctx = lax.axis_index("ctx")
    z = lax.axis_index("grp")
    c = lax.rem(ctx, NC)
    x = lax.rem(lax.div(ctx, NC), NX)
    y = lax.div(ctx, NC * NX)
    oc = 1 - c

    def at(yy, xx, cc, zz):
        return ((yy * NX + xx) * NC + cc, zz)

    def zpeer(d):
        return lax.rem(z + d, NZ)

    def xpeer(d):
        return lax.rem(x + d, NX)

    def ypeer(d):
        return lax.rem(y + d, NY)

    barrier = pltpu.get_barrier_semaphore()
    peers = [at(y, x, c, zpeer(d)) for d in range(1, NZ)]
    peers += [at(y, x, oc, z)]
    peers += [at(y, xpeer(d), c, z) for d in range(1, NX)]
    peers += [at(ypeer(d), x, c, z) for d in range(1, NY)]
    for peer in peers:
        pl.semaphore_signal(barrier, inc=1, device_id=peer, device_id_type=MESH)

    def lanes(head, width):
        return pl.ds(pl.multiple_of(head * width, width), width)

    def rows_of(zz):
        both = lanes(zz, 2 * D)
        return [pltpu.make_async_copy(q_hbm.at[:, both], qb.at[zz], ins.at[0, zz]),
                pltpu.make_async_copy(k_hbm.at[:, both], kb.at[zz], ins.at[1, zz])]

    def values_of(zz, part):
        copies = []
        for j in range(2):
            one = lanes(SHARE * zz + 2 * j + part, D)
            slot = 2 * zz + part
            copies.append(pltpu.make_async_copy(v_hbm.at[:, one], vb.at[slot, j], ins.at[2 + j, slot]))
            copies.append(pltpu.make_async_copy(go_hbm.at[:, one], gob.at[slot, j], ins.at[4 + j, slot]))
        return copies

    def outputs_of(zz, part):
        copies = []
        for j in range(2):
            one = lanes(SHARE * zz + 2 * j + part, D)
            slot = 2 * zz + part
            copies.append(pltpu.make_async_copy(outb.at[slot, j], out_hbm.at[:, one], outs.at[2 + j, slot]))
            copies.append(pltpu.make_async_copy(gvb.at[slot, j], gv_hbm.at[:, one], outs.at[4 + j, slot]))
        return copies

    def grads_of(zz):
        both = lanes(zz, 2 * D)
        return [pltpu.make_async_copy(gqb.at[zz], gq_hbm.at[:, both], outs.at[0, zz]),
                pltpu.make_async_copy(gkb.at[zz], gk_hbm.at[:, both], outs.at[1, zz])]

    def load_start(i, _):
        d, part = place(i)
        zz = zpeer(d)

        @pl.when(part == 0)
        def _():
            for copy in rows_of(zz):
                copy.start()

        for copy in values_of(zz, part):
            copy.start()
        return 0

    lax.fori_loop(0, NZ * PARTS, load_start, 0)
    for zz in range(NZ):
        for part in range(PARTS):
            for j in range(2):
                h = SHARE * zz + 2 * j + part
                ldp[2 * zz + part, j : j + 1] = ld_ref[h : h + 1]
                blp[2 * zz + part, j : j + 1] = bl_ref[h : h + 1]

    def remote(src, dst, send, recv, peer):
        return pltpu.make_async_remote_copy(
            src_ref=src, dst_ref=dst, send_sem=send, recv_sem=recv, device_id=peer, device_id_type=MESH)

    def zcopy(d, part):
        to = zpeer(d)
        return remote(tri.at[2 * to + part], zin.at[part, z], zs.at[d - 1, part], zr.at[d - 1, part], at(y, x, c, to))

    def ccopy(part):
        return remote(cout.at[part], cin.at[part, c], cs.at[part], cr.at[part], at(y, x, oc, z))

    def xcopy(d, part):
        return remote(xout.at[part, xpeer(d)], xin.at[part, x], xs.at[d - 1, part], xr.at[d - 1, part],
                      at(y, xpeer(d), c, z))

    def ycopy(d, part):
        return remote(yin.at[part, y], yin.at[part, y], ys.at[d - 1, part], yr.at[d - 1, part],
                      at(ypeer(d), x, c, z))

    def xdcopy(d, part):
        return remote(xdo.at[part, xpeer(d)], xdi.at[part, x], xds.at[d - 1, part], xdr.at[d - 1, part],
                      at(y, xpeer(d), c, z))

    def cdcopy(part):
        return remote(cdo.at[part, oc], cdi.at[part], cds.at[part], cdr.at[part], at(y, x, oc, z))

    def zdcopy(d, part, half):
        to = zpeer(d)
        core = lax.rem(c + half, NC)
        pair = NC * part + half
        return remote(zdo.at[part, to, core], sgin.at[part, z, core], zds.at[d - 1, pair], zdr.at[d - 1, pair],
                      at(y, x, c, to))

    def triple(ref):
        return ref[0], ref[1], ref[2]

    def packed(ref):
        return ref[0:D], ref[D : D + QUARTER], ref[D + QUARTER : D + 2 * QUARTER]

    def join_z(part):
        zin[part, z] = tri[2 * z + part]
        for d in range(1, NZ):
            zcopy(d, part).wait_recv()
        got = join_all([triple(zin.at[part, m, oc]) for m in range(NZ)])
        for i in range(3):
            cout[part, i] = got[i]
        ccopy(part).start()
        got = join_all([triple(zin.at[part, m, c]) for m in range(NZ)])
        for i in range(3):
            cin[part, c, i] = got[i]

    def join_core(part):
        ccopy(part).wait_recv()
        a, b, g = join_all([triple(cin.at[part, m]) for m in range(NC)])
        for to in range(NX):
            rows = slice(to * QUARTER, (to + 1) * QUARTER)
            xout[part, to, 0:D] = a
            xout[part, to, D : D + QUARTER] = b[rows]
            xout[part, to, D + QUARTER : D + 2 * QUARTER] = g[rows]
        for d in (2, 1, 3):
            xcopy(d, part).start()
        xin[part, x] = xout[part, x]

    def join_x(part):
        for d in range(1, NX):
            xcopy(d, part).wait_recv()
        row = join_all([packed(xin.at[part, m]) for m in range(NX)])
        yin[part, y, 0:D] = row[0]
        yin[part, y, D : D + QUARTER] = row[1]
        yin[part, y, D + QUARTER : D + 2 * QUARTER] = row[2]
        for d in (2, 1, 3):
            ycopy(d, part).start()

    def down_x(part):
        for d in range(1, NY):
            ycopy(d, part).wait_recv()
        zero = jnp.zeros((QUARTER, D), F32)
        states, grads = chain([packed(yin.at[part, m]) for m in range(NY)], zero, zero)
        state, grad = states[0], grads[0]
        for m in range(1, NY):
            state = jnp.where(y == m, states[m], state)
            grad = jnp.where(y == m, grads[m], grad)
        states, grads = chain([packed(xin.at[part, m]) for m in range(NX)], state, grad)
        for m in range(NX):
            xdo[part, m, 0:QUARTER] = states[m]
            xdo[part, m, QUARTER : 2 * QUARTER] = grads[m]
        for d in (2, 1, 3):
            xdcopy(d, part).start()
        xdi[part, x] = xdo[part, x]

    def down_core(part):
        for d in range(1, NX):
            xdcopy(d, part).wait_recv()
        state = jnp.concatenate([xdi[part, m, 0:QUARTER] for m in range(NX)], axis=0)
        grad = jnp.concatenate([xdi[part, m, QUARTER : 2 * QUARTER] for m in range(NX)], axis=0)
        states, grads = chain([triple(cin.at[part, m]) for m in range(NC)], state, grad)
        for m in range(NC):
            cdo[part, m, 0] = states[m]
            cdo[part, m, 1] = grads[m]
        cdcopy(part).start()

    def down_z(part):
        def one(core, state, grad):
            states, grads = chain([triple(zin.at[part, m, core]) for m in range(NZ)], state, grad)
            for m in range(NZ):
                zdo[part, m, core, 0] = states[m]
                zdo[part, m, core, 1] = grads[m]

        one(c, cdo[part, c, 0], cdo[part, c, 1])
        for d in (2, 1, 3):
            zdcopy(d, part, 0).start()
        cdcopy(part).wait_recv()
        one(oc, cdi[part, 0], cdi[part, 1])
        for d in (2, 1, 3):
            zdcopy(d, part, 1).start()
        sgin[part, z] = zdo[part, z]

    def up(i, _):
        d, part = place(i)
        zz = zpeer(d)
        slot = 2 * zz + part

        @pl.when(part == 0)
        def _():
            for copy in rows_of(zz):
                copy.wait()

        for copy in values_of(zz, part):
            copy.wait()
        phase1(qb.at[zz], kb.at[zz], vb.at[slot], gob.at[slot], ldp.at[slot], blp.at[slot], tri.at[slot],
               t_ref.at[slot], m_ref.at[slot], gam_ref.at[slot], u_ref.at[slot], w_ref.at[slot], r_ref.at[slot],
               aux_ref.at[slot], end_ref.at[slot])

        @pl.when(i == 0)
        def _():
            pl.semaphore_wait(barrier, len(peers))

        @pl.when(lax.rem(i, NZ) < NZ - 1)
        def _():
            zcopy(d, part).start()

        for step, stage in UP_STAGES:
            @pl.when(i == step)
            def _():
                stage_of[stage](0)

        return 0

    stage_of = dict(z=join_z, core=join_core, x=join_x, dx=down_x, dcore=down_core, dz=down_z)
    lax.fori_loop(0, NZ * PARTS, up, 0)
    for stage, part in MIDDLE:
        stage_of[stage](part)

    def down(i, _):
        d, part = place(lax.rem(i, NZ) + NZ - 1)
        part = lax.div(i, NZ)
        for step, stage in DOWN_STAGES:
            @pl.when(i == step)
            def _():
                stage_of[stage](1)

        @pl.when(lax.rem(i, NZ) > 0)
        def _():
            zdcopy(d, part, 0).wait_recv()
            zdcopy(d, part, 1).wait_recv()

        zz = lax.rem(z + NZ - d, NZ)
        slot = 2 * zz + part
        phase3(part, qb.at[zz], kb.at[zz], vb.at[slot], gob.at[slot], blp.at[slot], sgin.at[part, zz],
               t_ref.at[slot], m_ref.at[slot], gam_ref.at[slot], u_ref.at[slot], w_ref.at[slot], r_ref.at[slot],
               aux_ref.at[slot], end_ref.at[slot],
               outb.at[slot], gqb.at[zz], gkb.at[zz], gvb.at[slot], gdp.at[slot], gbp.at[slot])
        for copy in outputs_of(zz, part):
            copy.start()

        @pl.when(part == PARTS - 1)
        def _():
            for copy in grads_of(zz):
                copy.start()

        return 0

    lax.fori_loop(0, NZ * PARTS, down, 0)
    for zz in range(NZ):
        for part in range(PARTS):
            for j in range(2):
                h = SHARE * zz + 2 * j + part
                gd_ref[h : h + 1] = gdp[2 * zz + part, j : j + 1]
                gb_ref[h : h + 1] = gbp[2 * zz + part, j : j + 1]

    for part in range(PARTS):
        for d in range(1, NZ):
            zcopy(d, part).wait_send()
            zdcopy(d, part, 0).wait_send()
            zdcopy(d, part, 1).wait_send()
            xcopy(d, part).wait_send()
            xdcopy(d, part).wait_send()
            ycopy(d, part).wait_send()
        ccopy(part).wait_send()
        cdcopy(part).wait_send()

    def store_wait(zz, _):
        for copy in grads_of(zz):
            copy.wait()
        for part in range(PARTS):
            for copy in outputs_of(zz, part):
                copy.wait()
        return 0

    lax.fori_loop(0, NZ, store_wait, 0)


UP_STAGES = ((5, "z"), (6, "core"), (7, "x"))
MIDDLE = (("dx", 0), ("z", 1), ("core", 1), ("dcore", 0), ("dz", 0), ("x", 1))
DOWN_STAGES = ((1, "dx"), (2, "dcore"), (2, "dz"))


def run_layer(q, k, v, go, ld, bl):
    dma = pltpu.SemaphoreType.DMA

    def vm(*shape, dtype=F32):
        return pltpu.VMEM(shape, dtype)

    hbm = pl.BlockSpec(memory_space=pl.ANY)
    vmem = pl.BlockSpec(memory_space=pltpu.VMEM)
    slots = NZ * PARTS
    piece = D + 2 * QUARTER
    return pl.pallas_call(
        layer_kernel,
        in_specs=[hbm] * 4 + [vmem] * 2,
        out_specs=[hbm] * 4 + [vmem] * 2,
        out_shape=[
            jax.ShapeDtypeStruct((TOK, HEADS * D), F32),
            jax.ShapeDtypeStruct((TOK, KHEADS * D), F32),
            jax.ShapeDtypeStruct((TOK, KHEADS * D), F32),
            jax.ShapeDtypeStruct((TOK, HEADS * D), F32),
            jax.ShapeDtypeStruct((HEADS, TOK), F32),
            jax.ShapeDtypeStruct((HEADS, TOK), F32),
        ],
        scratch_shapes=[
            vm(NZ, TOK, 2 * D, dtype=BF16), vm(NZ, TOK, 2 * D, dtype=BF16),
            vm(slots, 2, TOK, D, dtype=BF16), vm(slots, 2, TOK, D, dtype=BF16),
            vm(slots, 2, TOK), vm(slots, 2, TOK), vm(slots, 2, TOK), vm(slots, 2, TOK),
            vm(slots, 2, 2, TOK, TOK, dtype=BF16), vm(slots, 2, 2, TOK, TOK, dtype=BF16), vm(slots, 2, TOK, TOK),
            vm(slots, 2, TOK, D), vm(slots, 2, 2, TOK, D, dtype=BF16), vm(slots, 2, D, TOK),
            vm(slots, TOK, D), vm(slots, 2, 8, D),
            vm(slots, NC, 3, D, D), vm(PARTS, NZ, NC, 3, D, D),
            vm(PARTS, 3, D, D), vm(PARTS, NC, 3, D, D),
            vm(PARTS, NX, piece, D), vm(PARTS, NX, piece, D), vm(PARTS, NY, piece, D),
            vm(PARTS, NX, 2 * QUARTER, D), vm(PARTS, NX, 2 * QUARTER, D),
            vm(PARTS, NC, 2, D, D), vm(PARTS, 2, D, D),
            vm(PARTS, NZ, NC, 2, D, D), vm(PARTS, NZ, NC, 2, D, D),
            vm(slots, 2, TOK, D), vm(NZ, TOK, 2 * D), vm(NZ, TOK, 2 * D), vm(slots, 2, TOK, D),
            dma((6, slots)), dma((6, slots)),
            dma((NZ - 1, PARTS)), dma((NZ - 1, PARTS)), dma((PARTS,)), dma((PARTS,)),
            dma((NX - 1, PARTS)), dma((NX - 1, PARTS)), dma((NY - 1, PARTS)), dma((NY - 1, PARTS)),
            dma((NX - 1, PARTS)), dma((NX - 1, PARTS)), dma((PARTS,)), dma((PARTS,)),
            dma((NZ - 1, NC * PARTS)), dma((NZ - 1, NC * PARTS)),
        ],
        compiler_params=pltpu.CompilerParams(
            collective_id=0, has_side_effects=True, vmem_limit_bytes=VMEM_LIMIT),
        name="delta_layer",
    )(q, k, v, go, ld, bl)


def hand_over(*refs):
    n = len(refs) // 2
    for i in range(n):
        refs[n + i][...] = refs[i][...]


def run_hand_over(arrays):
    steps = 4
    specs = [pl.BlockSpec((TOK // steps, a.shape[1]), lambda i: (i, 0)) for a in arrays[:4]]
    specs += [pl.BlockSpec((HEADS, TOK), lambda i: (0, 0))] * 2
    return pl.pallas_call(
        hand_over,
        grid=(steps,),
        in_specs=specs,
        out_specs=specs,
        out_shape=[jax.ShapeDtypeStruct(a.shape, a.dtype) for a in arrays],
        compiler_params=pltpu.CompilerParams(vmem_limit_bytes=VMEM_LIMIT),
        name="results",
    )(*arrays)


def on_device(query_rows, key_rows, value_rows, log_decay, beta_logit, grad_out):
    return tuple(run_hand_over(run_layer(query_rows, key_rows, value_rows, grad_out, log_decay, beta_logit)))


def solution(mesh):
    rows = P(("ctx", "grp"), None)
    heads = P(None, ("ctx", "grp"))
    return jax.shard_map(
        on_device,
        mesh=mesh,
        in_specs=(rows, rows, rows, heads, heads, rows),
        out_specs=(rows, rows, rows, rows, heads, heads),
        check_vma=False,
    )
```

```python
import jax
import jax.numpy as jnp
from jax import lax
from jax.experimental import pallas as pl
from jax.experimental.pallas import tpu as pltpu
from jax.sharding import PartitionSpec as P

F32 = jnp.float32
BF16 = jnp.bfloat16
TOK = 256
D = 128
HEADS = 16
KHEADS = 8


def dg(a, b, ca, cb):
    return lax.dot_general(a, b, (((ca,), (cb,)), ((), ())), preferred_element_type=F32)


def split(x):
    hi = x.astype(BF16)
    return hi, (x - hi.astype(F32)).astype(BF16)


def halves(both):
    n = both.shape[1] // 2
    return both[:, :n] + both[:, n:]


def dot4(a, b, ca, cb):
    wide = jnp.concatenate(b, axis=1 - cb)
    return halves(dg(jnp.concatenate(a, axis=ca), jnp.concatenate([wide, wide], axis=cb), ca, cb))


def dot2r(a, b, ca, cb):
    return halves(dg(a, jnp.concatenate(b, axis=1 - cb), ca, cb))


def dot2l(a, b, ca, cb):
    return dg(a[0], b, ca, cb) + dg(a[1], b, ca, cb)


def dot3(a, b, ca, cb):
    return dot2r(a[0], b, ca, cb) + dg(a[1], b[0], ca, cb)


def iota(shape, dim):
    return lax.broadcasted_iota(jnp.int32, shape, dim)


def cumulate(rows, tri):
    hi = rows.astype(BF16)
    rest = rows - hi.astype(F32)
    mid = rest.astype(BF16)
    low = (rest - mid.astype(F32)).astype(BF16)
    parts = jnp.concatenate([hi.astype(F32), mid.astype(F32), low.astype(F32), jnp.zeros((2, TOK), F32)], axis=0)
    got = dg(parts.astype(BF16), tri, 1, 0)
    return got[0:2] + (got[2:4] + got[4:6])


def invert(systems):
    n = len(systems)
    lane = iota((16, D), 1)
    row = iota((16, D), 0)
    block = lane // 16
    packed = []
    for mat in systems:
        got = jnp.where(block == 0, mat[0:16], 0.0)
        for i in range(1, 8):
            got = jnp.where(block == i, mat[16 * i : 16 * i + 16], got)
        packed.append(got)
    inv = [jnp.where(lane % 16 == row, 1.0, 0.0).astype(F32) for _ in range(n)]
    for m in range(15):
        index = block * 16 + m
        for c in range(n):
            column = jnp.take_along_axis(packed[c], index, axis=1, mode="promise_in_bounds")
            inv[c] = inv[c] - column * inv[c][m : m + 1, :]
    wide_r = iota((D, D), 0)
    wide_c = iota((D, D), 1)
    full = [
        jnp.concatenate([jnp.where(block == i, inv[c], 0.0) for i in range(8)], axis=0)
        for c in range(n)
    ]
    for b in (16, 32, 64):
        mask = (wide_r // (2 * b) == wide_c // (2 * b)) & (wide_r // b % 2 == 1) & (wide_c // b % 2 == 0)
        sides = [split(jnp.where(mask, systems[c], 0.0)) for c in range(n)]
        ts = [split(full[c]) for c in range(n)]
        inner = [split(dot4(sides[c], ts[c], 1, 0)) for c in range(n)]
        full = [full[c] - dot4(ts[c], inner[c], 1, 0) for c in range(n)]
    return full


def rows_to_cols(rows8):
    return jnp.concatenate([rows8] * 16, axis=0).T


def cols_to_rows(cols):
    lane = iota((TOK, D), 1)
    got = jnp.zeros((TOK, D), F32)
    for i, col in enumerate(cols):
        got = jnp.where(lane == i, col, got)
    return got.T


VMEM_LIMIT = 60 * 1024 * 1024


def phase1(q_ref, k_ref, v_ref, go_ref, ld_ref, bl_ref,
           tri_ref, t_ref, m_ref, gam_ref, u_ref, w_ref, r_ref, aux_ref, end_ref):
    both = range(2)
    t_i = iota((TOK, TOK), 0)
    s_i = iota((TOK, TOK), 1)
    upper = jnp.where(t_i <= s_i, 1.0, 0.0).astype(BF16)
    within = t_i >= s_i
    q = [q_ref[:, j * D : (j + 1) * D] for j in both]
    k = [k_ref[:, j * D : (j + 1) * D] for j in both]
    kk = [dg(k[j], k[j], 1, 1) for j in both]
    qk = [dg(q[j], k[j], 1, 1) for j in both]
    run = cumulate(ld_ref[...], upper)
    beta_rows = 1.0 / (1.0 + jnp.exp(-bl_ref[...]))
    last = run[:, TOK - 1 : TOK]
    grown = jnp.exp(run)
    cols = rows_to_cols(jnp.concatenate([run, beta_rows, grown, jnp.exp(last - run)], axis=0))
    lane = iota((TOK, D), 1)
    kf = [part.astype(F32) for part in k]
    for j in both:
        for i, part in ((8, q[j].astype(F32)), (10, kf[j])):
            norm = lax.rsqrt(jnp.sum(part * part, axis=1, keepdims=True) + 1e-6)
            cols = jnp.where(lane == i + j, norm, cols)
    aux_ref[...] = cols
    norm_rows = cols.T
    rq = [cols[:, 8 + j : 9 + j] for j in both]
    rk = [cols[:, 10 + j : 11 + j] for j in both]
    g = [cols[:, 4 + j : 5 + j] for j in both]
    frk = [cols[:, 6 + j : 7 + j] * rk[j] for j in both]
    gam = [jnp.exp(jnp.where(within, cols[:, j : j + 1] - run[j : j + 1], -1e30)) * norm_rows[10 + j : 11 + j]
           for j in both]
    systems = [jnp.where(t_i > s_i, kk[j] * gam[j] * (cols[:, 2 + j : 3 + j] * rk[j]), 0.0) for j in both]
    blocks = []
    for j in both:
        blocks += [systems[j][:D, :D], systems[j][D:, D:]]
    mix = [split(qk[j] * gam[j] * rq[j]) for j in both]
    go_t = [go_ref[j].T for j in both]
    r_t = [dg(go_t[j], mix[j][0], 1, 0) + dg(go_t[j], mix[j][1], 1, 0) for j in both]
    for j in both:
        gam_ref[j] = gam[j]
        m_ref[j, 0] = mix[j][0]
        m_ref[j, 1] = mix[j][1]
        r_ref[j] = r_t[j]
    inv = [split(block) for block in invert(blocks)]
    inner = [split(dot4(split(systems[j][D:, :D]), inv[2 * j], 1, 0)) for j in both]
    t21 = [split(-dot4(inv[2 * j + 1], inner[j], 1, 0)) for j in both]
    tb = []
    for j in both:
        whole = []
        for i in range(2):
            t11, t22 = inv[2 * j][i], inv[2 * j + 1][i]
            whole.append(jnp.concatenate(
                [jnp.concatenate([t11, jnp.zeros((D, D), BF16)], axis=1),
                 jnp.concatenate([t21[j][i], t22], axis=1)], axis=0))
        tb.append(split((whole[0].astype(F32) + whole[1].astype(F32)) * beta_rows[j : j + 1]))
    ks = [split(kf[j] * (g[j] * rk[j])) for j in both]
    uw = [dot2l(tb[j], jnp.concatenate([v_ref[j], ks[j][0]], axis=1), 1, 0) for j in both]
    w = [uw[j][:, D:] + dg(tb[j][0], ks[j][1], 1, 0) for j in both]
    ws = [split(w[j]) for j in both]
    ends = [jnp.exp(last[j : j + 1]) for j in both]
    ab = [dot2r(k[j].T, split(jnp.concatenate([w[j] * frk[j], uw[j][:, :D] * frk[j]], axis=1)), 1, 0) for j in both]
    go_g = [split(go_t[j].astype(F32) * (grown[j : j + 1] * norm_rows[8 + j : 9 + j])) for j in both]
    offset = [dot2l(go_g[j], q[j], 1, 0) for j in both]
    offset = [offset[j] - dot3(split(r_t[j]), ws[j], 1, 0) for j in both]
    eye = jnp.where(iota((D, D), 0) == iota((D, D), 1), 1.0, 0.0)
    for j in both:
        tri_ref[j, 0] = eye * ends[j] - ab[j][:, :D]
        tri_ref[j, 1] = ab[j][:, D:].T
        tri_ref[j, 2] = offset[j]
        t_ref[j, 0] = tb[j][0]
        t_ref[j, 1] = tb[j][1]
        u_ref[j] = uw[j][:, :D]
        w_ref[j, 0] = ws[j][0]
        w_ref[j, 1] = ws[j][1]
        end_ref[j] = jnp.broadcast_to(ends[j], (8, D))


def phase3(part, q_ref, k_ref, v_ref, go_ref, bl_ref, sg_ref, t_ref, m_ref, gam_ref, u_ref, w_ref, r_ref, aux_ref,
           end_ref, out_ref, gq_ref, gk_ref, gv_ref, gd_ref, gb_ref):
    both = range(2)
    aux = aux_ref[...]
    aux_rows = aux.T
    frk_rows = aux_rows[6:8] * aux_rows[10:12]
    t_i = iota((TOK, TOK), 0)
    s_i = iota((TOK, TOK), 1)
    strict = t_i > s_i
    lower = jnp.where(t_i >= s_i, 1.0, 0.0).astype(BF16)
    q = [q_ref[:, j * D : (j + 1) * D] for j in both]
    k = [k_ref[:, j * D : (j + 1) * D] for j in both]
    v = [v_ref[j] for j in both]
    go = [go_ref[j] for j in both]
    rq = [aux[:, 8 + j : 9 + j] for j in both]
    rk = [aux[:, 10 + j : 11 + j] for j in both]
    g = [aux[:, 4 + j : 5 + j] for j in both]
    frk = [aux[:, 6 + j : 7 + j] * rk[j] for j in both]
    ss = [split(sg_ref[j, 0]) for j in both]
    gs = [split(sg_ref[j, 1]) for j in both]
    xw = [dot4((w_ref[j, 0], w_ref[j, 1]), ss[j], 1, 1) for j in both]
    kg = [dg(jnp.concatenate(gs[j], axis=0), k[j], 1, 1) for j in both]
    qs = [dot2r(q[j], ss[j], 1, 1) for j in both]
    gos = [dot2r(go[j], ss[j], 1, 0) for j in both]
    x = [u_ref[j] - xw[j] for j in both]
    xs = [split(x[j]) for j in both]
    dx_t = [split(r_ref[j] + (kg[j][:D] + kg[j][D:]) * frk_rows[j : j + 1]) for j in both]
    y_t = [dg(dx_t[j][0], t_ref[j, 0], 1, 0) + (dg(dx_t[j][0], t_ref[j, 1], 1, 0) + dg(dx_t[j][1], t_ref[j, 0], 1, 0))
           for j in both]
    gx = [dg(jnp.concatenate([go[j], go[j]], axis=1), jnp.concatenate(xs[j], axis=1), 1, 1) for j in both]
    y = [y_t[j].T for j in both]
    ys = [split(y[j]) for j in both]
    for j in both:
        gv_ref[j] = y[j]
    mx = [dot3((m_ref[j, 0], m_ref[j, 1]), xs[j], 1, 0) for j in both]
    n = [split(gx[j] * gam_ref[j] * rq[j]) for j in both]
    yx = [dg(jnp.concatenate(ys[j], axis=1), jnp.concatenate([xs[j][0], xs[j][0]], axis=1), 1, 1)
          + dg(ys[j][0], xs[j][1], 1, 1) for j in both]
    out = [qs[j] * (g[j] * rq[j]) + mx[j] for j in both]
    for j in both:
        out_ref[j] = out[j]
    k_t = [k[j].T for j in both]
    q_t = [q[j].T for j in both]
    xk = [dot2r(k_t[j], split(x[j] * frk[j]), 1, 0) for j in both]
    ends = [jnp.sum(sg_ref[j, 1] * (sg_ref[j, 0] * end_ref[j][0:1] + xk[j].T), keepdims=True) for j in both]
    turned = [dg(q_t[j], n[j][0], 1, 0) + dg(q_t[j], n[j][1], 1, 0) for j in both]
    eq = [dot2l(n[j], k[j], 1, 0) for j in both]
    p = [split(jnp.where(strict, yx[j] * gam_ref[j] * (-rk[j]), 0.0)) for j in both]
    turned = [turned[j] + (dg(k_t[j], p[j][0], 1, 0) + dg(k_t[j], p[j][1], 1, 0)) for j in both]
    ek = [dot2l(p[j], k[j], 1, 0) for j in both]
    xg = [dot4(xs[j], gs[j], 1, 0) for j in both]
    sy = [dot4(ys[j], ss[j], 1, 0) for j in both]
    eq = [eq[j] + gos[j] * (g[j] * rq[j]) for j in both]
    ek = [ek[j] + turned[j].T + (xg[j] * frk[j] - sy[j] * (g[j] * rk[j])) for j in both]
    dots = [jnp.sum(go[j].astype(F32) * out[j] - v[j].astype(F32) * y[j], axis=1, keepdims=True) for j in both]
    dots += [jnp.sum(y[j] * x[j], axis=1, keepdims=True) for j in both]

    @pl.when(part == 0)
    def _():
        for j in both:
            gq_ref[:, j * D : (j + 1) * D] = eq[j]
            gk_ref[:, j * D : (j + 1) * D] = ek[j]

    @pl.when(part == 1)
    def _():
        for j in both:
            cols = slice(j * D, (j + 1) * D)
            for raw, ref, row, norm in ((q[j], gq_ref, eq[j], rq[j]), (k[j], gk_ref, ek[j], rk[j])):
                row = row + ref[:, cols]
                raw = raw.astype(F32)
                ref[:, cols] = row - raw * (norm * norm * jnp.sum(raw * row, axis=1, keepdims=True))

    rows = cols_to_rows(dots)
    suffix = cumulate(rows[0:2], lower)
    gd_ref[...] = suffix + jnp.concatenate(ends, axis=0)
    gb_ref[...] = jnp.exp(-bl_ref[...]) * rows[2:4]


MESH = pl.DeviceIdType.MESH
NZ, NC, NX, NY = 4, 2, 4, 4
SHARE = HEADS // NZ
PARTS = 2
QUARTER = D // NX


def join_all(parts):
    while len(parts) > 1:
        early, late = parts[0::2], parts[1::2]
        n = range(len(early))
        late_a = [split(p[0]) for p in late]
        late_c = [split(p[2]) for p in late]
        early_a = [split(p[0]) for p in early]
        early_b = [split(p[1]) for p in early]
        left = [[jnp.concatenate([a, g], axis=0) for a, g in zip(late_a[i], late_c[i])] for i in n]
        down = [dot4(left[i], early_a[i], 1, 0) for i in n]
        up = [dot4(early_b[i], late_a[i], 1, 1) for i in n]
        parts = [(down[i][:D], up[i] + late[i][1], down[i][D:] + early[i][2]) for i in n]
    return parts[0]


def chain(parts, state, grad):
    split_a = [split(p[0]) for p in parts]
    n = len(parts)
    states = [state]
    grads = [grad]
    for i in range(n - 1):
        ss, gs = split(states[-1]), split(grads[-1])
        moved = dot4(ss, split_a[i], 1, 1)
        back = dot4(gs, split_a[n - 1 - i], 1, 0)
        states.append(moved + parts[i][1])
        grads.append(back + parts[n - 1 - i][2])
    return states, grads[::-1]


def place(i):
    r = lax.rem(i, NZ)
    return lax.rem(lax.div(3 * r * r + 4 - 5 * r, 2), NZ), lax.div(i, NZ)


def layer_kernel(q_hbm, k_hbm, v_hbm, go_hbm, ld_ref, bl_ref,
                 out_hbm, gq_hbm, gk_hbm, gv_hbm, gd_ref, gb_ref,
                 qb, kb, vb, gob, ldp, blp, gdp, gbp, t_ref, m_ref, gam_ref, u_ref, w_ref, r_ref, aux_ref, end_ref,
                 tri, zin, cout, cin, xout, xin, yin, xdo, xdi, cdo, cdi, zdo, sgin,
                 outb, gqb, gkb, gvb,
                 ins, outs, zs, zr, cs, cr, xs, xr, ys, yr, xds, xdr, cds, cdr, zds, zdr):
    ctx = lax.axis_index("ctx")
    z = lax.axis_index("grp")
    c = lax.rem(ctx, NC)
    x = lax.rem(lax.div(ctx, NC), NX)
    y = lax.div(ctx, NC * NX)
    oc = 1 - c

    def at(yy, xx, cc, zz):
        return ((yy * NX + xx) * NC + cc, zz)

    def zpeer(d):
        return lax.rem(z + d, NZ)

    def xpeer(d):
        return lax.rem(x + d, NX)

    def ypeer(d):
        return lax.rem(y + d, NY)

    barrier = pltpu.get_barrier_semaphore()
    peers = [at(y, x, c, zpeer(d)) for d in range(1, NZ)]
    peers += [at(y, x, oc, z)]
    peers += [at(y, xpeer(d), c, z) for d in range(1, NX)]
    peers += [at(ypeer(d), x, c, z) for d in range(1, NY)]
    for peer in peers:
        pl.semaphore_signal(barrier, inc=1, device_id=peer, device_id_type=MESH)

    def lanes(head, width):
        return pl.ds(pl.multiple_of(head * width, width), width)

    def rows_of(zz):
        both = lanes(zz, 2 * D)
        return [pltpu.make_async_copy(q_hbm.at[:, both], qb.at[zz], ins.at[0, zz]),
                pltpu.make_async_copy(k_hbm.at[:, both], kb.at[zz], ins.at[1, zz])]

    def values_of(zz, part):
        copies = []
        for j in range(2):
            one = lanes(SHARE * zz + 2 * j + part, D)
            slot = 2 * zz + part
            copies.append(pltpu.make_async_copy(v_hbm.at[:, one], vb.at[slot, j], ins.at[2 + j, slot]))
            copies.append(pltpu.make_async_copy(go_hbm.at[:, one], gob.at[slot, j], ins.at[4 + j, slot]))
        return copies

    def outputs_of(zz, part):
        copies = []
        for j in range(2):
            one = lanes(SHARE * zz + 2 * j + part, D)
            slot = 2 * zz + part
            copies.append(pltpu.make_async_copy(outb.at[slot, j], out_hbm.at[:, one], outs.at[2 + j, slot]))
            copies.append(pltpu.make_async_copy(gvb.at[slot, j], gv_hbm.at[:, one], outs.at[4 + j, slot]))
        return copies

    def grads_of(zz):
        both = lanes(zz, 2 * D)
        return [pltpu.make_async_copy(gqb.at[zz], gq_hbm.at[:, both], outs.at[0, zz]),
                pltpu.make_async_copy(gkb.at[zz], gk_hbm.at[:, both], outs.at[1, zz])]

    def load_start(i, _):
        d, part = place(i)
        zz = zpeer(d)

        @pl.when(part == 0)
        def _():
            for copy in rows_of(zz):
                copy.start()

        for copy in values_of(zz, part):
            copy.start()
        return 0

    lax.fori_loop(0, NZ * PARTS, load_start, 0)
    for zz in range(NZ):
        for part in range(PARTS):
            for j in range(2):
                h = SHARE * zz + 2 * j + part
                ldp[2 * zz + part, j : j + 1] = ld_ref[h : h + 1]
                blp[2 * zz + part, j : j + 1] = bl_ref[h : h + 1]

    def remote(src, dst, send, recv, peer):
        return pltpu.make_async_remote_copy(
            src_ref=src, dst_ref=dst, send_sem=send, recv_sem=recv, device_id=peer, device_id_type=MESH)

    def zcopy(d, part):
        to = zpeer(d)
        return remote(tri.at[2 * to + part], zin.at[part, z], zs.at[d - 1, part], zr.at[d - 1, part], at(y, x, c, to))

    def ccopy(part):
        return remote(cout.at[part], cin.at[part, c], cs.at[part], cr.at[part], at(y, x, oc, z))

    def xcopy(d, part):
        return remote(xout.at[part, xpeer(d)], xin.at[part, x], xs.at[d - 1, part], xr.at[d - 1, part],
                      at(y, xpeer(d), c, z))

    def ycopy(d, part):
        return remote(yin.at[part, y], yin.at[part, y], ys.at[d - 1, part], yr.at[d - 1, part],
                      at(ypeer(d), x, c, z))

    def xdcopy(d, part):
        return remote(xdo.at[part, xpeer(d)], xdi.at[part, x], xds.at[d - 1, part], xdr.at[d - 1, part],
                      at(y, xpeer(d), c, z))

    def cdcopy(part):
        return remote(cdo.at[part, oc], cdi.at[part], cds.at[part], cdr.at[part], at(y, x, oc, z))

    def zdcopy(d, part, half):
        to = zpeer(d)
        core = lax.rem(c + half, NC)
        pair = NC * part + half
        return remote(zdo.at[part, to, core], sgin.at[part, z, core], zds.at[d - 1, pair], zdr.at[d - 1, pair],
                      at(y, x, c, to))

    def triple(ref):
        return ref[0], ref[1], ref[2]

    def packed(ref):
        return ref[0:D], ref[D : D + QUARTER], ref[D + QUARTER : D + 2 * QUARTER]

    def join_z(part):
        zin[part, z] = tri[2 * z + part]
        for d in range(1, NZ):
            zcopy(d, part).wait_recv()
        got = join_all([triple(zin.at[part, m, oc]) for m in range(NZ)])
        for i in range(3):
            cout[part, i] = got[i]
        ccopy(part).start()
        got = join_all([triple(zin.at[part, m, c]) for m in range(NZ)])
        for i in range(3):
            cin[part, c, i] = got[i]

    def join_core(part):
        ccopy(part).wait_recv()
        a, b, g = join_all([triple(cin.at[part, m]) for m in range(NC)])
        for to in range(NX):
            rows = slice(to * QUARTER, (to + 1) * QUARTER)
            xout[part, to, 0:D] = a
            xout[part, to, D : D + QUARTER] = b[rows]
            xout[part, to, D + QUARTER : D + 2 * QUARTER] = g[rows]
        for d in (2, 1, 3):
            xcopy(d, part).start()
        xin[part, x] = xout[part, x]

    def join_x(part):
        for d in range(1, NX):
            xcopy(d, part).wait_recv()
        row = join_all([packed(xin.at[part, m]) for m in range(NX)])
        yin[part, y, 0:D] = row[0]
        yin[part, y, D : D + QUARTER] = row[1]
        yin[part, y, D + QUARTER : D + 2 * QUARTER] = row[2]
        for d in (2, 1, 3):
            ycopy(d, part).start()

    def down_x(part):
        for d in range(1, NY):
            ycopy(d, part).wait_recv()
        zero = jnp.zeros((QUARTER, D), F32)
        states, grads = chain([packed(yin.at[part, m]) for m in range(NY)], zero, zero)
        state, grad = states[0], grads[0]
        for m in range(1, NY):
            state = jnp.where(y == m, states[m], state)
            grad = jnp.where(y == m, grads[m], grad)
        states, grads = chain([packed(xin.at[part, m]) for m in range(NX)], state, grad)
        for m in range(NX):
            xdo[part, m, 0:QUARTER] = states[m]
            xdo[part, m, QUARTER : 2 * QUARTER] = grads[m]
        for d in (2, 1, 3):
            xdcopy(d, part).start()
        xdi[part, x] = xdo[part, x]

    def down_core(part):
        for d in range(1, NX):
            xdcopy(d, part).wait_recv()
        state = jnp.concatenate([xdi[part, m, 0:QUARTER] for m in range(NX)], axis=0)
        grad = jnp.concatenate([xdi[part, m, QUARTER : 2 * QUARTER] for m in range(NX)], axis=0)
        states, grads = chain([triple(cin.at[part, m]) for m in range(NC)], state, grad)
        for m in range(NC):
            cdo[part, m, 0] = states[m]
            cdo[part, m, 1] = grads[m]
        cdcopy(part).start()

    def down_z(part):
        def one(core, state, grad):
            states, grads = chain([triple(zin.at[part, m, core]) for m in range(NZ)], state, grad)
            for m in range(NZ):
                zdo[part, m, core, 0] = states[m]
                zdo[part, m, core, 1] = grads[m]

        one(c, cdo[part, c, 0], cdo[part, c, 1])
        for d in (2, 1, 3):
            zdcopy(d, part, 0).start()
        cdcopy(part).wait_recv()
        one(oc, cdi[part, 0], cdi[part, 1])
        for d in (2, 1, 3):
            zdcopy(d, part, 1).start()
        sgin[part, z] = zdo[part, z]

    def up(i, _):
        d, part = place(i)
        zz = zpeer(d)
        slot = 2 * zz + part

        @pl.when(part == 0)
        def _():
            for copy in rows_of(zz):
                copy.wait()

        for copy in values_of(zz, part):
            copy.wait()
        phase1(qb.at[zz], kb.at[zz], vb.at[slot], gob.at[slot], ldp.at[slot], blp.at[slot], tri.at[slot],
               t_ref.at[slot], m_ref.at[slot], gam_ref.at[slot], u_ref.at[slot], w_ref.at[slot], r_ref.at[slot],
               aux_ref.at[slot], end_ref.at[slot])

        @pl.when(i == 0)
        def _():
            pl.semaphore_wait(barrier, len(peers))

        @pl.when(lax.rem(i, NZ) < NZ - 1)
        def _():
            zcopy(d, part).start()

        for step, stage in UP_STAGES:
            @pl.when(i == step)
            def _():
                stage_of[stage](0)

        return 0

    stage_of = dict(z=join_z, core=join_core, x=join_x, dx=down_x, dcore=down_core, dz=down_z)
    lax.fori_loop(0, NZ * PARTS, up, 0)
    for stage, part in MIDDLE:
        stage_of[stage](part)

    def down(i, _):
        d, part = place(lax.rem(i, NZ) + NZ - 1)
        part = lax.div(i, NZ)
        for step, stage in DOWN_STAGES:
            @pl.when(i == step)
            def _():
                stage_of[stage](1)

        @pl.when(lax.rem(i, NZ) > 0)
        def _():
            zdcopy(d, part, 0).wait_recv()
            zdcopy(d, part, 1).wait_recv()

        zz = lax.rem(z + NZ - d, NZ)
        slot = 2 * zz + part
        phase3(part, qb.at[zz], kb.at[zz], vb.at[slot], gob.at[slot], blp.at[slot], sgin.at[part, zz],
               t_ref.at[slot], m_ref.at[slot], gam_ref.at[slot], u_ref.at[slot], w_ref.at[slot], r_ref.at[slot],
               aux_ref.at[slot], end_ref.at[slot],
               outb.at[slot], gqb.at[zz], gkb.at[zz], gvb.at[slot], gdp.at[slot], gbp.at[slot])
        for copy in outputs_of(zz, part):
            copy.start()

        @pl.when(part == PARTS - 1)
        def _():
            for copy in grads_of(zz):
                copy.start()

        return 0

    lax.fori_loop(0, NZ * PARTS, down, 0)
    for zz in range(NZ):
        for part in range(PARTS):
            for j in range(2):
                h = SHARE * zz + 2 * j + part
                gd_ref[h : h + 1] = gdp[2 * zz + part, j : j + 1]
                gb_ref[h : h + 1] = gbp[2 * zz + part, j : j + 1]

    for part in range(PARTS):
        for d in range(1, NZ):
            zcopy(d, part).wait_send()
            zdcopy(d, part, 0).wait_send()
            zdcopy(d, part, 1).wait_send()
            xcopy(d, part).wait_send()
            xdcopy(d, part).wait_send()
            ycopy(d, part).wait_send()
        ccopy(part).wait_send()
        cdcopy(part).wait_send()

    def store_wait(zz, _):
        for copy in grads_of(zz):
            copy.wait()
        for part in range(PARTS):
            for copy in outputs_of(zz, part):
                copy.wait()
        return 0

    lax.fori_loop(0, NZ, store_wait, 0)


UP_STAGES = ((5, "z"), (6, "core"), (7, "x"))
MIDDLE = (("dx", 0), ("z", 1), ("dcore", 0), ("core", 1), ("dz", 0), ("x", 1))
DOWN_STAGES = ((1, "dx"), (2, "dcore"), (2, "dz"))


def run_layer(q, k, v, go, ld, bl):
    dma = pltpu.SemaphoreType.DMA

    def vm(*shape, dtype=F32):
        return pltpu.VMEM(shape, dtype)

    hbm = pl.BlockSpec(memory_space=pl.ANY)
    vmem = pl.BlockSpec(memory_space=pltpu.VMEM)
    slots = NZ * PARTS
    piece = D + 2 * QUARTER
    return pl.pallas_call(
        layer_kernel,
        in_specs=[hbm] * 4 + [vmem] * 2,
        out_specs=[hbm] * 4 + [vmem] * 2,
        out_shape=[
            jax.ShapeDtypeStruct((TOK, HEADS * D), F32),
            jax.ShapeDtypeStruct((TOK, KHEADS * D), F32),
            jax.ShapeDtypeStruct((TOK, KHEADS * D), F32),
            jax.ShapeDtypeStruct((TOK, HEADS * D), F32),
            jax.ShapeDtypeStruct((HEADS, TOK), F32),
            jax.ShapeDtypeStruct((HEADS, TOK), F32),
        ],
        scratch_shapes=[
            vm(NZ, TOK, 2 * D, dtype=BF16), vm(NZ, TOK, 2 * D, dtype=BF16),
            vm(slots, 2, TOK, D, dtype=BF16), vm(slots, 2, TOK, D, dtype=BF16),
            vm(slots, 2, TOK), vm(slots, 2, TOK), vm(slots, 2, TOK), vm(slots, 2, TOK),
            vm(slots, 2, 2, TOK, TOK, dtype=BF16), vm(slots, 2, 2, TOK, TOK, dtype=BF16), vm(slots, 2, TOK, TOK),
            vm(slots, 2, TOK, D), vm(slots, 2, 2, TOK, D, dtype=BF16), vm(slots, 2, D, TOK),
            vm(slots, TOK, D), vm(slots, 2, 8, D),
            vm(slots, NC, 3, D, D), vm(PARTS, NZ, NC, 3, D, D),
            vm(PARTS, 3, D, D), vm(PARTS, NC, 3, D, D),
            vm(PARTS, NX, piece, D), vm(PARTS, NX, piece, D), vm(PARTS, NY, piece, D),
            vm(PARTS, NX, 2 * QUARTER, D), vm(PARTS, NX, 2 * QUARTER, D),
            vm(PARTS, NC, 2, D, D), vm(PARTS, 2, D, D),
            vm(PARTS, NZ, NC, 2, D, D), vm(PARTS, NZ, NC, 2, D, D),
            vm(slots, 2, TOK, D), vm(NZ, TOK, 2 * D), vm(NZ, TOK, 2 * D), vm(slots, 2, TOK, D),
            dma((6, slots)), dma((6, slots)),
            dma((NZ - 1, PARTS)), dma((NZ - 1, PARTS)), dma((PARTS,)), dma((PARTS,)),
            dma((NX - 1, PARTS)), dma((NX - 1, PARTS)), dma((NY - 1, PARTS)), dma((NY - 1, PARTS)),
            dma((NX - 1, PARTS)), dma((NX - 1, PARTS)), dma((PARTS,)), dma((PARTS,)),
            dma((NZ - 1, NC * PARTS)), dma((NZ - 1, NC * PARTS)),
        ],
        compiler_params=pltpu.CompilerParams(
            collective_id=0, has_side_effects=True, vmem_limit_bytes=VMEM_LIMIT),
        name="delta_layer",
    )(q, k, v, go, ld, bl)


def hand_over(*refs):
    n = len(refs) // 2
    for i in range(n):
        refs[n + i][...] = refs[i][...]


def run_hand_over(arrays):
    steps = 2
    specs = [pl.BlockSpec((TOK // steps, a.shape[1]), lambda i: (i, 0)) for a in arrays[:4]]
    specs += [pl.BlockSpec((HEADS, TOK), lambda i: (0, 0))] * 2
    return pl.pallas_call(
        hand_over,
        grid=(steps,),
        in_specs=specs,
        out_specs=specs,
        out_shape=[jax.ShapeDtypeStruct(a.shape, a.dtype) for a in arrays],
        compiler_params=pltpu.CompilerParams(vmem_limit_bytes=VMEM_LIMIT),
        name="results",
    )(*arrays)


def on_device(query_rows, key_rows, value_rows, log_decay, beta_logit, grad_out):
    return tuple(run_hand_over(run_layer(query_rows, key_rows, value_rows, grad_out, log_decay, beta_logit)))


def solution(mesh):
    rows = P(("ctx", "grp"), None)
    heads = P(None, ("ctx", "grp"))
    return jax.shard_map(
        on_device,
        mesh=mesh,
        in_specs=(rows, rows, rows, heads, heads, rows),
        out_specs=(rows, rows, rows, rows, heads, heads),
        check_vma=False,
    )
```
